128 devices in a mesh: dom: 8 (over y, z_lo), grp: 16 (over z_hi, x, core).
Axes of the slice: x: 4, y: 4, z: 4 (z_hi: 2, z_lo: 2; z = z_hi * 2 + z_lo), core: 2. Of those that a mesh axis runs over, the one named last changes fastest.
Arguments:
- states: float32 [262144, 128], P(('dom', 'grp')), may hold values from -6 to 6
- potential: float32 [262144], P(('dom', 'grp')), may hold values from 0.3 to 3
- cell_scale: float32 [32768], P(('dom', 'grp')), may hold values from 0.25 to 1
- stiffness: float32 [27, 27], replicated
- connect: int32 [27, 32768], P(None, ('dom', 'grp')), may hold values from 0 to 2559, as said below
- face_nodes: int32 [2, 32768], P(None, ('dom', 'grp')), may hold values from 0 to 2047, as said below
- node_count: int32 [128], P(('dom', 'grp')), may hold values from 512 to 2048, as said below
- filter_cut: float32 [1], replicated, may hold values from 8 to 20
- spectrum_top: float32 [1], replicated, may hold values from 100 to 160
Outputs:
- ortho_states: float32 [262144, 128], P(('dom', 'grp'))
- projected: float32 [512, 32], P('grp')
The draws below stay inside these ranges and needn't reach their ends.
Inputs may be any that keep to these rules, and one draw needn't show every extreme that they name: `connect`: cell k of a domain lies in cell block b = k // 32 and references only rows of the extended list that are lower ghosts (0 .. 255), upper ghosts (2304 and above), or owned slots s (row 256 + s) with min(b, 6) * 256 <= s < min(b, 6) * 256 + 2 * 256; owned slots referenced by live cells are below the domain's node count. `face_nodes`: indices of live node slots of the domain; within one domain the lower and the upper lists each hold distinct nodes. `node_count`: A multiple of 32; some domain has exactly 2048.
All inputs are finite; a program needn't handle non-finite values.
Results may differ from the reference program's by a relative error of at most 0.0003.
Values sent between devices are 32-bit elements; how exact they have to be, the bound alone decides.
A program may use at most 128 MiB of HBM per device.

```python
import math
import jax
import jax.numpy as jnp
from jax import lax

NB = 8
NS = 128
NPC = 27
DEG = 4
NODES_DEV = 2048
CELLS_DEV = 256
FACE = 256
NODES = 262144
CELLS = 32768
PR = 4
PC = 4
TILE_R = 32
TILE_C = 32
N_GRP = 16
DEVICES = 128


def node_counts(key):
    key = jax.random.fold_in(key, 11)
    first, second = jax.random.split(key)
    counts = 32 * jax.random.randint(first, (DEVICES,), NODES_DEV // 128, NODES_DEV // 32 + 1)
    fullest = jax.random.randint(second, (), 0, DEVICES)
    return jnp.where(jnp.arange(DEVICES) == fullest, NODES_DEV, counts).astype(jnp.int32)


def draw_node_count(key, part):
    return node_counts(key)


def draw_face_nodes(key, part):
    counts = node_counts(key)
    key = jax.random.fold_in(key, 5)
    first, second = jax.random.split(key)
    low_keys = jax.random.split(first, DEVICES)
    high_keys = jax.random.split(second, DEVICES)
    lower = jax.vmap(lambda single: jax.random.permutation(single, FACE))(low_keys).astype(jnp.int32)
    orders = jax.vmap(lambda single: jax.random.permutation(single, FACE))(high_keys).astype(jnp.int32)
    upper = counts[:, None] - FACE + orders
    return jnp.stack([lower.reshape(-1), upper.reshape(-1)]).astype(jnp.int32)


def draw_connect(key, part):
    counts = node_counts(key)
    key = jax.random.fold_in(key, 7)
    first, second, third = jax.random.split(key, 3)
    cell = jnp.arange(CELLS_DEV, dtype=jnp.int32)[None, None, :]
    slot = jnp.arange(NPC, dtype=jnp.int32)[None, :, None]
    block_index = cell // (FACE // 8)
    start = jnp.minimum(block_index, 6) * FACE
    span = jnp.clip(counts[:, None, None] - start, 1, 2 * FACE)
    raw = jax.random.randint(first, (DEVICES, NPC, CELLS_DEV), 0, 2 * FACE)
    owned = FACE + start + raw % span
    ghost_low = jax.random.randint(second, (DEVICES, NPC, CELLS_DEV), 0, FACE)
    ghost_high = FACE + NODES_DEV + jax.random.randint(third, (DEVICES, NPC, CELLS_DEV), 0, FACE)
    ghost_low = jnp.where((cell == 0) & (slot == 0), 0, ghost_low)
    ghost_high = jnp.where((cell == 1) & (slot == 0), NODES_DEV + 2 * FACE - 1, ghost_high)
    boundary = (cell < FACE // 8) & (slot < 9)
    ghost = jnp.where(cell % 2 == 0, ghost_low, ghost_high)
    chosen = jnp.where(boundary, ghost, owned)
    return chosen.transpose(1, 0, 2).reshape(NPC, DEVICES * CELLS_DEV).astype(jnp.int32)


def draw_stiffness(key, part):
    key = jax.random.fold_in(key, 3)
    first, second = jax.random.split(key)
    off = 0.1 * jax.random.normal(first, (NPC, NPC), jnp.float32)
    eye = jnp.eye(NPC, dtype=jnp.float32)
    off = (off + off.T) * 0.5 * (1.0 - eye)
    diag = jnp.sum(jnp.abs(off), axis=1) + jax.random.uniform(second, (NPC,), jnp.float32, 0.5, 1.5)
    return off + diag[:, None] * eye


def shard_levels(rng, dims, cuts, smallest, top_value):
    gain = 1.0
    for dim, shards_of in cuts:
        draws = jax.random.uniform(jax.random.fold_in(jax.random.fold_in(rng, 6), dim), (shards_of,), jnp.float32, smallest / len(cuts), top_value / len(cuts))
        gain = gain * jnp.repeat(jnp.exp(draws), dims[dim] // shards_of).reshape((-1,) + (1,) * (len(dims) - 1 - dim))
    return gain


def scatter_about(rng, extent, scale, bound, pieces=(), kind=jnp.bfloat16):
    level = shard_levels(rng, extent, pieces, -0.22, 0.18) if pieces else 1.0
    entries = jax.random.normal(rng, extent, jnp.float32) * scale * level
    return jnp.minimum(jnp.maximum(entries, -bound), bound).astype(kind)


def setup_inputs(seed: int = 0) -> dict:
    keys = jax.random.split(jax.random.key(seed), 10)
    return {
        "states": scatter_about(keys[0], (NODES, NS), 1.0, 6.0, ((0, 128),), jnp.float32),
        "potential": jnp.clip(jnp.exp(math.log(3.0) - 2.3025851 * jax.random.uniform(keys[1], (NODES,), jnp.float32) ** shard_levels(keys[1], (NODES,), ((0, 128),), -0.2, 0.2)), 0.3, 3.0),
        "cell_scale": jnp.clip(jnp.exp(math.log(1.0) - 1.3862944 * jax.random.uniform(keys[2], (CELLS,), jnp.float32) ** shard_levels(keys[2], (CELLS,), ((0, 128),), -0.2, 0.2)), 0.25, 1.0),
        "stiffness": draw_stiffness(jax.random.fold_in(keys[9], 71), 0),
        "connect": draw_connect(jax.random.fold_in(keys[9], 71), 0),
        "face_nodes": draw_face_nodes(jax.random.fold_in(keys[9], 71), 0),
        "node_count": draw_node_count(jax.random.fold_in(keys[9], 71), 0),
        "filter_cut": jnp.clip(jax.random.uniform(keys[7], (1,), jnp.float32, 8.0, 20.0), 8.0, 20.0),
        "spectrum_top": jnp.clip(jax.random.uniform(keys[8], (1,), jnp.float32, 100.0, 160.0), 100.0, 160.0),
    }


HIGH = lax.Precision.HIGHEST

def cell_terms(ext, conn, scale, stiffness):
    gathered = jnp.take(ext, conn, axis=0)
    local = jnp.einsum('ab,bcv->acv', stiffness, gathered, precision=HIGH) * scale[None, :, None]
    empty = jnp.zeros(ext.shape, jnp.float32)
    return empty.at[conn.reshape(-1)].add(local.reshape(-1, ext.shape[1]))

def apply_all(field, potential, scale, stiffness, connect, lower, upper):
    take_rows = jax.vmap(lambda block, index: jnp.take(block, index, axis=0))
    lows = take_rows(field, lower)
    highs = take_rows(field, upper)
    zero = jnp.zeros_like(lows[:1])
    below = jnp.concatenate([zero, highs[:-1]], axis=0)
    above = jnp.concatenate([lows[1:], zero], axis=0)
    ext = jnp.concatenate([below, field, above], axis=1)

    def one_domain(items):
        return cell_terms(items[0], items[1], items[2], stiffness)
    out = lax.map(one_domain, (ext, connect, scale))
    own = out[:, FACE:FACE + NODES_DEV] + potential[:, :, None] * field
    low_part = out[:, :FACE]
    high_part = out[:, FACE + NODES_DEV:]
    from_below = jnp.concatenate([zero, high_part[:-1]], axis=0)
    from_above = jnp.concatenate([low_part[1:], zero], axis=0)
    add_rows = jax.vmap(lambda block, index, values: block.at[index].add(values))
    own = add_rows(own, lower, from_below)
    own = add_rows(own, upper, from_above)
    return own

def arrange(full, rows_grid, cols_grid, block):
    size = full.shape[0]
    tiles = full.reshape(size // (rows_grid * block), rows_grid, block, size // (cols_grid * block), cols_grid, block)
    tiles = tiles.transpose(1, 4, 0, 2, 3, 5)
    return tiles.reshape(rows_grid * cols_grid, size // rows_grid, size // cols_grid)

def reference(states, potential, cell_scale, stiffness, connect, face_nodes, node_count, filter_cut, spectrum_top):
    field = states.reshape(DEVICES, NODES_DEV, NS)
    node_mask = (jnp.arange(NODES_DEV, dtype=jnp.int32)[None, :] < node_count[:, None]).astype(jnp.float32)
    cell_mask = (jnp.arange(CELLS_DEV, dtype=jnp.int32)[None, :] < (node_count // 8)[:, None]).astype(jnp.float32)
    scale = cell_scale.reshape(DEVICES, CELLS_DEV) * cell_mask
    conn = connect.reshape(NPC, DEVICES, CELLS_DEV).transpose(1, 0, 2)
    lower = face_nodes[0].reshape(DEVICES, FACE)
    upper = face_nodes[1].reshape(DEVICES, FACE)
    pot = potential.reshape(DEVICES, NODES_DEV)

    def hamil(v):
        return apply_all(v, pot, scale, stiffness, conn, lower, upper)
    half = (spectrum_top[0] - filter_cut[0]) * 0.5
    centre = (spectrum_top[0] + filter_cut[0]) * 0.5
    previous = field * node_mask[:, :, None]
    current = (hamil(previous) - centre * previous) / half
    for step in range(DEG - 1):
        following = 2.0 * (hamil(current) - centre * current) / half - previous
        previous, current = (current, following)
    filtered = current.reshape(NODES, NS)
    hfiltered = hamil(current).reshape(NODES, NS)
    correlation = jnp.dot(filtered.T, filtered, precision=HIGH) / NODES
    hgram = jnp.dot(filtered.T, hfiltered, precision=HIGH) / NODES
    factor = jnp.linalg.cholesky(correlation)
    inverse = jax.scipy.linalg.solve_triangular(factor, jnp.eye(NS, dtype=jnp.float32), lower=True)
    ortho_states = jnp.dot(filtered, inverse.T, precision=HIGH)
    hhat = jnp.dot(jnp.dot(inverse, hgram, precision=HIGH), inverse.T, precision=HIGH)
    projected = arrange(hhat, PR, PC, NB).reshape(N_GRP * TILE_R, TILE_C)
    return (ortho_states, projected)
```

```python
import functools

import jax
import jax.numpy as jnp
from jax import lax
from jax.experimental import pallas as pl
from jax.experimental.pallas import tpu as pltpu
from jax.sharding import PartitionSpec as P

NB = 8
NS = 128
NPC = 27
SLOTS = 28
DEG = 4
COUNT = 2048
FACE = 256
BLOCKS = 8
GROUPS = 4
GROWS = SLOTS * 8
ROWS = GROUPS * GROWS
WIN = 2 * FACE
GHOST = 2 * FACE

F32 = jnp.float32
BF16 = jnp.bfloat16
MESH = pl.DeviceIdType.MESH


def dot(a, b, dims=((1,), (0,))):
    return lax.dot_general(a, b, (dims, ((), ())), preferred_element_type=F32)


def split(x):
    hi = x.astype(BF16)
    lo = (x - hi.astype(F32)).astype(BF16)
    return jnp.concatenate([hi, lo], axis=1)


def halves(x):
    return x[:, :NS] + x[:, NS:]


def quarters(x):
    return (x[:NS, :NS] + x[NS:, NS:]) + (x[:NS, NS:] + x[NS:, :NS])


def filter_kernel(
    n_dom,
    n_grp,
    cut_ref,
    top_ref,
    live_ref,
    states_ref,
    pot_ref,
    scale_ref,
    kmat_ref,
    connr_ref,
    connc_ref,
    facer_ref,
    facec_ref,
    f_ref,
    corr_ref,
    hgram_ref,
    g_own,
    g_gho,
    t_own,
    t_gho,
    pick,
    pick_t,
    kk_hi,
    kk_lo,
    gath,
    loc,
    ext,
    extg,
    prev,
    work,
    face_send,
    face_recv,
    back_send,
    back_recv,
    ar_src,
    ar_slots,
    ar_part,
    ar_doms,
    ar_out,
    face_sems,
    back_sems,
    ar_sems1,
    ar_sems2,
    ar_sems3,
):
    dom = lax.axis_index("dom")
    grp = lax.axis_index("grp")
    total = n_dom * n_grp
    me = dom * n_grp + grp
    up = lax.rem(me + 1, total)
    down = lax.rem(me + total - 1, total)
    up_id = (up // n_grp, lax.rem(up, n_grp))
    down_id = (down // n_grp, lax.rem(down, n_grp))
    partners = [up_id, down_id]
    partners += [(dom, lax.rem(grp + s, n_grp)) for s in range(1, n_grp)]
    partners += [(lax.rem(dom + s, n_dom), grp) for s in range(1, n_dom)]
    barrier = pltpu.get_barrier_semaphore()
    for device in partners:
        pl.semaphore_signal(barrier, inc=1, device_id=device, device_id_type=MESH)

    def build(b, carry):
        lane8 = lax.broadcasted_iota(jnp.int32, (ROWS, BLOCKS), 1)
        col = jnp.sum(jnp.where(lane8 == b, connc_ref[...], 0), axis=1, keepdims=True)
        lane = lax.broadcasted_iota(jnp.int32, (ROWS, WIN), 1)
        g_own[b] = jnp.where(col == lane, 1.0, 0.0).astype(BF16)
        g_gho[b] = jnp.where(col == lane + WIN, 1.0, 0.0).astype(BF16)
        row = connr_ref[b]
        sub = lax.broadcasted_iota(jnp.int32, (WIN, ROWS), 0)
        t_own[b] = jnp.where(row == sub, 1.0, 0.0).astype(BF16)
        t_gho[:, pl.ds(pl.multiple_of(b * ROWS, 128), ROWS)] = jnp.where(
            row == sub + WIN, 1.0, 0.0
        ).astype(BF16)
        return carry

    lax.fori_loop(0, BLOCKS, build, 0)
    pick[...] = jnp.where(
        facec_ref[...] == lax.broadcasted_iota(jnp.int32, (2 * FACE, COUNT), 1), 1.0, 0.0
    ).astype(BF16)
    pick_t[...] = jnp.where(
        facer_ref[...] == lax.broadcasted_iota(jnp.int32, (COUNT, 2 * FACE), 0), 1.0, 0.0
    ).astype(BF16)
    spread = (
        lax.broadcasted_iota(jnp.int32, (GROWS, SLOTS), 0) // 8
        == lax.broadcasted_iota(jnp.int32, (GROWS, SLOTS), 1)
    )
    spread = jnp.where(spread, 1.0, 0.0).astype(F32)
    wide = lax.dot_general(
        spread, kmat_ref[...], (((1,), (0,)), ((), ())),
        precision=lax.Precision.HIGHEST, preferred_element_type=F32,
    )
    wide = lax.dot_general(
        wide, spread, (((1,), (1,)), ((), ())),
        precision=lax.Precision.HIGHEST, preferred_element_type=F32,
    )
    same = lax.rem(lax.broadcasted_iota(jnp.int32, (GROWS, GROWS), 0), 8) == lax.rem(
        lax.broadcasted_iota(jnp.int32, (GROWS, GROWS), 1), 8
    )
    wide = jnp.where(same, wide, 0.0)
    kk_hi[...] = wide.astype(BF16)
    kk_lo[...] = (wide - wide.astype(BF16).astype(F32)).astype(BF16)

    live = live_ref[0]
    rows = lax.broadcasted_iota(jnp.int32, (COUNT, NS), 0)
    f_ref[...] = jnp.where(rows < live, states_ref[...], 0.0)
    prev[...] = jnp.zeros((COUNT, NS), F32)
    half = (top_ref[0] - cut_ref[0]) * 0.5
    centre = (top_ref[0] + cut_ref[0]) * 0.5

    pl.semaphore_wait(barrier, len(partners))

    def exchange(send, recv, sems):
        down_copy = pltpu.make_async_remote_copy(
            src_ref=send.at[0], dst_ref=recv.at[1],
            send_sem=sems.at[0], recv_sem=sems.at[1],
            device_id=down_id, device_id_type=MESH,
        )
        up_copy = pltpu.make_async_remote_copy(
            src_ref=send.at[1], dst_ref=recv.at[0],
            send_sem=sems.at[2], recv_sem=sems.at[3],
            device_id=up_id, device_id_type=MESH,
        )
        down_copy.start()
        up_copy.start()
        return down_copy, up_copy

    def window(b):
        return pl.ds(pl.multiple_of(jnp.minimum(b, 6) * FACE, FACE), WIN)

    def load_field():
        def body(i, carry):
            at = pl.ds(pl.multiple_of(i * FACE, FACE), FACE)
            ext[at] = split(f_ref[at])
            return carry

        lax.fori_loop(0, COUNT // FACE, body, 0)

    def cells():
        load_field()
        sel = halves(dot(pick[...], ext[...]))
        face_send[0] = sel[:FACE]
        face_send[1] = sel[FACE:]
        copies = exchange(face_send, face_recv, face_sems)

        def owned(b, carry):
            gath[b] = dot(g_own[b], ext[window(b)]).astype(BF16)
            return carry

        lax.fori_loop(0, BLOCKS, owned, 0)
        for copy in copies:
            copy.wait()
        extg[0:FACE] = split(jnp.where(me == 0, 0.0, face_recv[0]))
        extg[FACE:] = split(jnp.where(me == total - 1, 0.0, face_recv[1]))

        def ghosts(b, carry):
            g = gath[b] + dot(g_gho[b], extg[...]).astype(BF16)
            for i in range(0, GROUPS, 2):
                one = g[i * GROWS : (i + 1) * GROWS]
                two = g[(i + 1) * GROWS : (i + 2) * GROWS]
                low = dot(kk_lo[...], jnp.concatenate([one[:, :NS], two[:, :NS]], axis=1))
                for j, part in enumerate((one, two)):
                    out = halves(dot(kk_hi[...], part)) + low[:, j * NS : (j + 1) * NS]
                    at = pl.ds(pl.multiple_of((b * GROUPS + i + j) * 8, 8), 8)
                    out = (out.reshape(SLOTS, 8, NS) * scale_ref[at][None]).reshape(GROWS, NS)
                    at = pl.ds(pl.multiple_of((b * GROUPS + i + j) * GROWS, 16), GROWS)
                    loc[at] = split(out)
            return carry

        lax.fori_loop(0, BLOCKS, ghosts, 0)

    def scatter_owned():
        work[...] = jnp.zeros((COUNT, NS), F32)

        def body(b, carry):
            at = pl.ds(pl.multiple_of(b * ROWS, 128), ROWS)
            work[window(b)] += halves(dot(t_own[b], loc[at]))
            return carry

        lax.fori_loop(0, BLOCKS, body, 0)

    def step(k, carry):
        alpha = jnp.where(k == 0, 1.0, 2.0) / half
        beta = jnp.where(k == 0, 0.0, 1.0)
        cells()
        back = halves(dot(t_gho[...], loc[...]))
        back_send[0] = back[:FACE]
        back_send[1] = back[FACE:]
        copies = exchange(back_send, back_recv, back_sems)
        scatter_owned()
        for copy in copies:
            copy.wait()
        extg[0:FACE] = split(jnp.where(me == 0, 0.0, back_recv[0]))
        extg[FACE:] = split(jnp.where(me == total - 1, 0.0, back_recv[1]))

        def body(i, carry):
            at = pl.ds(pl.multiple_of(i * FACE, FACE), FACE)
            added = work[at] + halves(dot(pick_t[at], extg[...]))
            cur = f_ref[at]
            new = alpha * (added + (pot_ref[at] - centre) * cur) - beta * prev[at]
            prev[at] = cur
            f_ref[at] = new
            return carry

        lax.fori_loop(0, COUNT // FACE, body, 0)
        return carry

    lax.fori_loop(0, DEG, step, 0)
    cells()
    corr = quarters(dot(ext[...], ext[...], ((0,), (0,))))
    scatter_owned()
    back = halves(dot(t_gho[...], loc[...]))
    hgram = quarters(dot(extg[...], split(back), ((0,), (0,))))

    def body(i, acc):
        at = pl.ds(pl.multiple_of(i * FACE, FACE), FACE)
        hf = work[at] + pot_ref[at] * f_ref[at]
        return acc + dot(ext[at], split(hf), ((0,), (0,)))

    acc = lax.fori_loop(0, COUNT // FACE, body, jnp.zeros((2 * NS, 2 * NS), F32))
    hgram = hgram + quarters(acc)

    inv_total = 1.0 / (total * COUNT)
    piece = NS // n_grp
    for j in range(n_grp):
        ar_src[j, :piece] = corr[j * piece : (j + 1) * piece] * inv_total
        ar_src[j, piece:] = hgram[j * piece : (j + 1) * piece] * inv_total
    copies = []
    for s in range(1, n_grp):
        other = lax.rem(grp + s, n_grp)
        copies.append(
            pltpu.make_async_remote_copy(
                src_ref=ar_src.at[other], dst_ref=ar_slots.at[s],
                send_sem=ar_sems1.at[0, s], recv_sem=ar_sems1.at[1, s],
                device_id=(dom, other), device_id_type=MESH,
            )
        )
    for copy in copies:
        copy.start()
    ar_slots[0] = ar_src[grp]
    for copy in copies:
        copy.wait()
    ar_part[...] = jnp.sum(ar_slots[...], axis=0)
    copies = []
    for s in range(1, n_dom):
        copies.append(
            pltpu.make_async_remote_copy(
                src_ref=ar_part, dst_ref=ar_doms.at[dom],
                send_sem=ar_sems2.at[0, s], recv_sem=ar_sems2.at[1, s],
                device_id=(lax.rem(dom + s, n_dom), grp), device_id_type=MESH,
            )
        )
    for copy in copies:
        copy.start()
    ar_doms[dom] = ar_part[...]
    for copy in copies:
        copy.wait()
    ar_part[...] = jnp.sum(ar_doms[...], axis=0)
    copies = []
    for s in range(1, n_grp):
        copies.append(
            pltpu.make_async_remote_copy(
                src_ref=ar_part, dst_ref=ar_out.at[grp],
                send_sem=ar_sems3.at[0, s], recv_sem=ar_sems3.at[1, s],
                device_id=(dom, lax.rem(grp + s, n_grp)), device_id_type=MESH,
            )
        )
    for copy in copies:
        copy.start()
    ar_out[grp] = ar_part[...]
    for copy in copies:
        copy.wait()
    for j in range(n_grp):
        corr_ref[j * piece : (j + 1) * piece] = ar_out[j, :piece]
        hgram_ref[j * piece : (j + 1) * piece] = ar_out[j, piece:]


def filtered_and_grams(n_dom, n_grp, operands):
    piece = NS // n_grp
    vmem = pl.BlockSpec(memory_space=pltpu.VMEM)
    smem = pl.BlockSpec(memory_space=pltpu.SMEM)
    dma = pltpu.SemaphoreType.DMA
    return pl.pallas_call(
        functools.partial(filter_kernel, n_dom, n_grp),
        out_shape=(
            jax.ShapeDtypeStruct((COUNT, NS), F32),
            jax.ShapeDtypeStruct((NS, NS), F32),
            jax.ShapeDtypeStruct((NS, NS), F32),
        ),
        in_specs=[smem] * 3 + [vmem] * 8,
        out_specs=(vmem, vmem, vmem),
        scratch_shapes=[
            pltpu.VMEM((BLOCKS, ROWS, WIN), BF16),
            pltpu.VMEM((BLOCKS, ROWS, GHOST), BF16),
            pltpu.VMEM((BLOCKS, WIN, ROWS), BF16),
            pltpu.VMEM((GHOST, BLOCKS * ROWS), BF16),
            pltpu.VMEM((2 * FACE, COUNT), BF16),
            pltpu.VMEM((COUNT, 2 * FACE), BF16),
            pltpu.VMEM((GROWS, GROWS), BF16),
            pltpu.VMEM((GROWS, GROWS), BF16),
            pltpu.VMEM((BLOCKS, ROWS, 2 * NS), BF16),
            pltpu.VMEM((BLOCKS * ROWS, 2 * NS), BF16),
            pltpu.VMEM((COUNT, 2 * NS), BF16),
            pltpu.VMEM((GHOST, 2 * NS), BF16),
            pltpu.VMEM((COUNT, NS), F32),
            pltpu.VMEM((COUNT, NS), F32),
            pltpu.VMEM((2, FACE, NS), F32),
            pltpu.VMEM((2, FACE, NS), F32),
            pltpu.VMEM((2, FACE, NS), F32),
            pltpu.VMEM((2, FACE, NS), F32),
            pltpu.VMEM((n_grp, 2 * piece, NS), F32),
            pltpu.VMEM((n_grp, 2 * piece, NS), F32),
            pltpu.VMEM((2 * piece, NS), F32),
            pltpu.VMEM((n_dom, 2 * piece, NS), F32),
            pltpu.VMEM((n_grp, 2 * piece, NS), F32),
            dma((4,)),
            dma((4,)),
            dma((2, n_grp)),
            dma((2, n_dom)),
            dma((2, n_grp)),
        ],
        compiler_params=pltpu.CompilerParams(
            collective_id=0, has_side_effects=True, vmem_limit_bytes=62 * 1024 * 1024
        ),
    )(*operands)


def finish_kernel(rows_grid, f_ref, corr_ref, hgram_ref, ortho_ref, tile_ref, inv_ref):
    grp = lax.axis_index("grp")
    sub = lax.broadcasted_iota(jnp.int32, (8, NS), 0)
    lane = lax.broadcasted_iota(jnp.int32, (8, NS), 1)
    panels = NS // 8
    high = lax.Precision.HIGHEST
    left = [corr_ref[8 * p : 8 * p + 8] for p in range(panels)]
    right = [jnp.where(lane == sub + 8 * p, 1.0, 0.0).astype(F32) for p in range(panels)]
    for p in range(panels):
        a, m = left[p], right[p]
        for j in range(8):
            c = 8 * p + j
            scale = 1.0 / jnp.sqrt(a[j : j + 1, c : c + 1])
            col = a[:, c : c + 1] * scale
            arow = a[j : j + 1] * scale
            mrow = m[j : j + 1] * scale
            a = jnp.where(sub > j, a - col * arow, jnp.where(sub == j, arow, a))
            m = jnp.where(sub > j, m - col * mrow, jnp.where(sub == j, mrow, m))
        inv_ref[8 * p : 8 * p + 8] = m
        if p + 1 < panels:
            both = lax.dot_general(
                a, jnp.concatenate([a, m], axis=1), (((0,), (0,)), ((), ())),
                precision=high, preferred_element_type=F32,
            )
            for q in range(p + 1, panels):
                left[q] = left[q] - both[8 * q : 8 * q + 8, :NS]
                right[q] = right[q] - both[8 * q : 8 * q + 8, NS:]
    inv = inv_ref[...]
    hi = inv.astype(BF16)
    lo = (inv - hi.astype(F32)).astype(BF16)
    wide = jnp.concatenate([hi, hi], axis=1)
    narrow = jnp.concatenate([lo, jnp.zeros_like(lo)], axis=1)
    weights = jnp.concatenate([wide, narrow], axis=0)

    def body(i, carry):
        at = pl.ds(pl.multiple_of(i * 256, 256), 256)
        ortho_ref[at] = halves(dot(split(f_ref[at]), weights, ((1,), (1,))))
        return carry

    lax.fori_loop(0, f_ref.shape[0] // 256, body, 0)
    r = grp // 4
    q = lax.rem(grp, 4)
    step = 8 * rows_grid
    mine = jnp.concatenate(
        [inv_ref[pl.ds(pl.multiple_of(step * t + 8 * r, 8), 8)] for t in range(NS // step)], axis=0
    )
    other = jnp.concatenate(
        [inv_ref[pl.ds(pl.multiple_of(32 * t + 8 * q, 8), 8)] for t in range(NS // 32)], axis=0
    )
    mine = jnp.dot(mine, hgram_ref[...], precision=high, preferred_element_type=F32)
    tile_ref[...] = lax.dot_general(
        mine, other, (((1,), (1,)), ((), ())), precision=high, preferred_element_type=F32
    )


def body(
    states,
    potential,
    cell_scale,
    stiffness,
    connect,
    face_nodes,
    node_count,
    filter_cut,
    spectrum_top,
):
    n_dom = lax.axis_size("dom")
    n_grp = lax.axis_size("grp")
    cells = cell_scale.shape[0]
    live_cells = node_count[0] // 8
    scale = jnp.where(jnp.arange(cells, dtype=jnp.int32) < live_cells, cell_scale, 0.0)
    scale = jnp.broadcast_to(scale[:, None], (cells, NS))
    pot = jnp.broadcast_to(potential[:, None], (COUNT, NS))
    start = jnp.minimum(jnp.arange(cells, dtype=jnp.int32) // 32, 6) * FACE
    column = jnp.where(
        connect < FACE,
        connect + WIN,
        jnp.where(connect >= FACE + COUNT, connect - FACE - COUNT + WIN + FACE, connect - FACE - start),
    )
    column = jnp.pad(column, ((0, SLOTS - NPC), (0, 0)), constant_values=-1)
    column = column.reshape(SLOTS, BLOCKS, GROUPS, 8).transpose(1, 2, 0, 3).reshape(BLOCKS, ROWS)
    kmat = jnp.pad(stiffness, ((0, SLOTS - NPC), (0, SLOTS - NPC)))
    f, corr, hgram = filtered_and_grams(
        n_dom,
        n_grp,
        (
            filter_cut,
            spectrum_top,
            node_count,
            states,
            pot,
            scale,
            kmat,
            column[:, None, :],
            column.T,
            face_nodes.reshape(1, -1),
            face_nodes.reshape(-1, 1),
        ),
    )
    rows_grid = n_grp // 4
    vmem = pl.BlockSpec(memory_space=pltpu.VMEM)
    return pl.pallas_call(
        functools.partial(finish_kernel, rows_grid),
        out_shape=(
            jax.ShapeDtypeStruct((COUNT, NS), F32),
            jax.ShapeDtypeStruct((NS // rows_grid, NS // 4), F32),
        ),
        in_specs=[vmem] * 3,
        out_specs=(vmem, vmem),
        scratch_shapes=[pltpu.VMEM((NS, NS), F32)],
        compiler_params=pltpu.CompilerParams(vmem_limit_bytes=32 * 1024 * 1024),
    )(f, corr, hgram)


def solution(mesh):
    placed = (
        P(("dom", "grp"), None),
        P(("dom", "grp")),
        P(("dom", "grp")),
        P(),
        P(None, ("dom", "grp")),
        P(None, ("dom", "grp")),
        P(("dom", "grp")),
        P(),
        P(),
    )
    return jax.shard_map(
        body,
        mesh=mesh,
        in_specs=placed,
        out_specs=(P(("dom", "grp"), None), P("grp", None)),
        check_vma=False,
    )
```

```python
import functools

import jax
import jax.numpy as jnp
from jax import lax
from jax.experimental import pallas as pl
from jax.experimental.pallas import tpu as pltpu
from jax.sharding import PartitionSpec as P

NB = 8
NS = 128
NPC = 27
SLOTS = 28
DEG = 4
COUNT = 2048
FACE = 256
BLOCKS = 8
GROUPS = 4
GROWS = SLOTS * 8
ROWS = GROUPS * GROWS
WIN = 2 * FACE
GHOST = 2 * FACE

F32 = jnp.float32
BF16 = jnp.bfloat16
MESH = pl.DeviceIdType.MESH


def dot(a, b, dims=((1,), (0,))):
    return lax.dot_general(a, b, (dims, ((), ())), preferred_element_type=F32)


def split(x):
    hi = x.astype(BF16)
    lo = (x - hi.astype(F32)).astype(BF16)
    return jnp.concatenate([hi, lo], axis=1)


def halves(x):
    return x[:, :NS] + x[:, NS:]


def quarters(x):
    return (x[:NS, :NS] + x[NS:, NS:]) + (x[:NS, NS:] + x[NS:, :NS])


CHUNK_BLOCKS = ((0, 1), (0, 2), (1, 3), (2, 4), (3, 5), (4, 6), (5, 8), (6, 8))
CHUNK_AT = (0, 1, 3, 5, 7, 9, 11, 14)
CHUNK_ALL = 16


class Sum:
    def __init__(self, n_dom, n_grp, dom, grp, refs):
        self.src, self.slots, self.part, self.doms, self.out, self.sems1, self.sems2, self.sems3 = refs
        self.n_dom, self.n_grp, self.dom, self.grp = n_dom, n_grp, dom, grp

    def grp_copy(self, s, src, dst, sems):
        return pltpu.make_async_remote_copy(
            src_ref=src, dst_ref=dst, send_sem=sems.at[0, s], recv_sem=sems.at[1, s],
            device_id=(self.dom, lax.rem(self.grp + s, self.n_grp)), device_id_type=MESH,
        )

    def first(self):
        return [
            self.grp_copy(s, self.src.at[lax.rem(self.grp + s, self.n_grp)], self.slots.at[s], self.sems1)
            for s in range(1, self.n_grp)
        ]

    def second(self):
        return [
            pltpu.make_async_remote_copy(
                src_ref=self.part.at[0], dst_ref=self.doms.at[self.dom],
                send_sem=self.sems2.at[0, s], recv_sem=self.sems2.at[1, s],
                device_id=(lax.rem(self.dom + s, self.n_dom), self.grp), device_id_type=MESH,
            )
            for s in range(1, self.n_dom)
        ]

    def third(self):
        return [
            self.grp_copy(s, self.part.at[1], self.out.at[self.grp], self.sems3)
            for s in range(1, self.n_grp)
        ]

    def start_first(self, value):
        piece = NS // self.n_grp
        for j in range(self.n_grp):
            self.src[j] = value[j * piece : (j + 1) * piece]
        for copy in self.first():
            copy.start()
        self.slots[0] = self.src[self.grp]

    def start_second(self):
        for copy in self.first():
            copy.wait()
        self.part[0] = jnp.sum(self.slots[...], axis=0)
        for copy in self.second():
            copy.start()
        self.doms[self.dom] = self.part[0]

    def start_third(self):
        for copy in self.second():
            copy.wait()
        self.part[1] = jnp.sum(self.doms[...], axis=0)
        for copy in self.third():
            copy.start()
        self.out[self.grp] = self.part[1]

    def finish(self):
        for copy in self.third():
            copy.wait()
        return self.out[...].reshape(NS, NS)


def triple(x):
    hi = x.astype(BF16).astype(F32)
    rest = x - hi
    mid = rest.astype(BF16).astype(F32)
    return hi, mid, rest - mid


def factor_panel(p, left_ref, right_ref):
    sub = lax.broadcasted_iota(jnp.int32, (8, NS), 0)
    rows = slice(8 * p, 8 * p + 8)
    a = left_ref[rows]
    m = right_ref[rows]
    cols = [jnp.broadcast_to(a[:, 8 * p + k : 8 * p + k + 1], (8, NS)) for k in range(8)]
    pivots = jnp.ones((8, NS), F32)
    for j in range(8):
        at = [None] * j + [jnp.broadcast_to(cols[k][j : j + 1], (8, NS)) for k in range(j, 8)]
        mult = jnp.where(sub > j, cols[j] * (1.0 / at[j]), 0.0)
        for k in range(j + 1, 8):
            cols[k] = cols[k] - mult * at[k]
        a, m = (
            a - mult * jnp.broadcast_to(a[j : j + 1], (8, NS)),
            m - mult * jnp.broadcast_to(m[j : j + 1], (8, NS)),
        )
        pivots = jnp.where(sub == j, at[j], pivots)
    scale = 1.0 / jnp.sqrt(pivots)
    a, m = a * scale, m * scale
    right_ref[rows] = m
    if 8 * p + 8 < NS:
        hi, mid, low = triple(a)
        mhi, mmid, mlow = triple(m)
        one = jnp.concatenate([hi, hi, mid, hi, low, mid], axis=0).astype(BF16)
        two = jnp.concatenate([hi, mid, hi, low, hi, mid], axis=0)
        two_m = jnp.concatenate([mhi, mmid, mhi, mlow, mhi, mmid], axis=0)
        two = jnp.concatenate([two, two_m], axis=1).astype(BF16)
        both = dot(one, two, ((0,), (0,)))
        rest = slice(8 * p + 8, NS)
        left_ref[rest] = left_ref[rest] - both[rest, :NS]
        right_ref[rest] = right_ref[rest] - both[rest, NS:]


def filter_kernel(
    n_dom,
    n_grp,
    cut_ref,
    top_ref,
    live_ref,
    states_ref,
    pot_ref,
    scale_ref,
    kmat_ref,
    conn_ref,
    face_ref,
    ortho_ref,
    tile_ref,
    g_own,
    g_gho,
    t_own,
    t_gho,
    pick,
    pick_t,
    cross,
    kk,
    gath,
    loc,
    ext,
    extg,
    cur,
    prev,
    pot,
    scale,
    face_part,
    face_send,
    face_recv,
    back_send,
    back_recv,
    left,
    right,
    face_sems,
    back_sems,
    *sums,
):
    dom = lax.axis_index("dom")
    grp = lax.axis_index("grp")
    total = n_dom * n_grp
    me = dom * n_grp + grp
    up = lax.rem(me + 1, total)
    down = lax.rem(me + total - 1, total)
    up_id = (up // n_grp, lax.rem(up, n_grp))
    down_id = (down // n_grp, lax.rem(down, n_grp))
    partners = [up_id, down_id]
    partners += [(dom, lax.rem(grp + s, n_grp)) for s in range(1, n_grp)]
    partners += [(lax.rem(dom + s, n_dom), grp) for s in range(1, n_dom)]
    barrier = pltpu.get_barrier_semaphore()
    for device in partners:
        pl.semaphore_signal(barrier, inc=1, device_id=device, device_id_type=MESH)
    corr_sum = Sum(n_dom, n_grp, dom, grp, sums[: len(sums) // 2])
    gram_sum = Sum(n_dom, n_grp, dom, grp, sums[len(sums) // 2 :])

    def pair(send, recv, sems):
        return (
            pltpu.make_async_remote_copy(
                src_ref=send.at[0], dst_ref=recv.at[1],
                send_sem=sems.at[0], recv_sem=sems.at[1],
                device_id=down_id, device_id_type=MESH,
            ),
            pltpu.make_async_remote_copy(
                src_ref=send.at[1], dst_ref=recv.at[0],
                send_sem=sems.at[2], recv_sem=sems.at[3],
                device_id=up_id, device_id_type=MESH,
            ),
        )

    def send_faces(values):
        face_send[0] = values[:FACE]
        face_send[1] = values[FACE:]
        for copy in pair(face_send, face_recv, face_sems):
            copy.start()

    def received(recv):
        low = jnp.where(me == 0, 0.0, recv[0])
        high = jnp.where(me == total - 1, 0.0, recv[1])
        return low, high

    live = live_ref[0]
    face_rows = jnp.concatenate([face_ref[:, :NS], face_ref[:, NS:]], axis=0).astype(F32)
    stacked = jnp.concatenate(
        [pot_ref[...], scale_ref[...], face_rows, jnp.zeros((2, NS), F32)], axis=0
    )
    columns = stacked.T
    for i, c in enumerate((18, 20, 19, 21)):
        want = columns[:, c : c + 1].astype(jnp.int32)
        lane = lax.broadcasted_iota(jnp.int32, (NS, COUNT), 1)
        pick[i * NS : (i + 1) * NS] = jnp.where(want == lane, 1.0, 0.0).astype(BF16)
    for i in range(0, COUNT, FACE):
        at = slice(i, i + FACE)
        node = lax.broadcasted_iota(jnp.int32, (FACE, NS), 0) + i
        cur[at] = jnp.where(node < live, states_ref[at], 0.0)
        ext[at] = split(cur[at])
    face_part[...] = halves(dot(pick[...], ext[...]))
    pl.semaphore_wait(barrier, len(partners))
    send_faces(face_part[...])

    conn = conn_ref[...]
    conn_col = conn.astype(F32).T.astype(jnp.int32)
    for b in range(BLOCKS):
        col = conn_col[:, b : b + 1]
        lane = lax.broadcasted_iota(jnp.int32, (ROWS, WIN), 1)
        g_own[b] = jnp.where(col == lane, 1.0, 0.0).astype(BF16)
        g_gho[b] = jnp.where(col == lane + WIN, 1.0, 0.0).astype(BF16)
        sub = lax.broadcasted_iota(jnp.int32, (GHOST, ROWS), 0)
        t_gho[:, b * ROWS : (b + 1) * ROWS] = jnp.where(conn[b : b + 1] == sub + WIN, 1.0, 0.0).astype(
            BF16
        )
    for j, (first, last) in enumerate(CHUNK_BLOCKS):
        for b in range(first, last):
            sub = lax.broadcasted_iota(jnp.int32, (FACE, ROWS), 0) + (j - min(b, 6)) * FACE
            at = CHUNK_AT[j] + b - first
            t_own[:, at * ROWS : (at + 1) * ROWS] = jnp.where(conn[b : b + 1] == sub, 1.0, 0.0).astype(
                BF16
            )
    for half_face in range(2):
        sub = lax.broadcasted_iota(jnp.int32, (COUNT, FACE), 0)
        pick_t[:, half_face * FACE : (half_face + 1) * FACE] = jnp.where(
            face_ref[half_face : half_face + 1] == sub, 1.0, 0.0
        ).astype(BF16)
    cross[...] = dot(pick[...], pick_t[...]).astype(BF16)
    spread = (
        lax.broadcasted_iota(jnp.int32, (GROWS, NPC), 0) // 8
        == lax.broadcasted_iota(jnp.int32, (GROWS, NPC), 1)
    )
    spread = jnp.where(spread, 1.0, 0.0).astype(F32)
    wide = lax.dot_general(
        spread, kmat_ref[...], (((1,), (0,)), ((), ())),
        precision=lax.Precision.HIGHEST, preferred_element_type=F32,
    )
    wide = lax.dot_general(
        wide, spread, (((1,), (1,)), ((), ())),
        precision=lax.Precision.HIGHEST, preferred_element_type=F32,
    )
    same = lax.rem(lax.broadcasted_iota(jnp.int32, (GROWS, GROWS), 0), 8) == lax.rem(
        lax.broadcasted_iota(jnp.int32, (GROWS, GROWS), 1), 8
    )
    wide = jnp.where(same, wide, 0.0)
    kk[0] = wide.astype(BF16)
    kk[1] = (wide - wide.astype(BF16).astype(F32)).astype(BF16)
    for i in range(COUNT // NS):
        pot[i * NS : (i + 1) * NS] = jnp.broadcast_to(columns[:, i : i + 1], (NS, NS))
    for i in range(2):
        cell = lax.broadcasted_iota(jnp.int32, (NS, NS), 0) + i * NS
        value = jnp.broadcast_to(columns[:, 16 + i : 17 + i], (NS, NS))
        scale[i * NS : (i + 1) * NS] = jnp.where(8 * cell + 8 <= live, value, 0.0)
    prev[...] = jnp.zeros((COUNT, NS), F32)
    span = (top_ref[0] - cut_ref[0]) * 0.5
    centre = (top_ref[0] + cut_ref[0]) * 0.5

    def gather_owned():
        for b in range(BLOCKS):
            at = min(b, 6) * FACE
            gath[b] = dot(g_own[b], ext[at : at + WIN]).astype(BF16)

    def gather_ghosts():
        for b in range(BLOCKS):
            gath[b] = gath[b] + dot(g_gho[b], extg[...]).astype(BF16)

    def take_faces():
        for copy in pair(face_send, face_recv, face_sems):
            copy.wait()
        low, high = received(face_recv)
        extg[:FACE] = split(low)
        extg[FACE:] = split(high)

    def apply_cells():
        for b in range(BLOCKS):
            for i in range(0, GROUPS, 2):
                one = gath[b, i * GROWS : (i + 1) * GROWS]
                two = gath[b, (i + 1) * GROWS : (i + 2) * GROWS]
                low = dot(kk[1], jnp.concatenate([one[:, :NS], two[:, :NS]], axis=1))
                for j, part in enumerate((one, two)):
                    r = b * GROUPS + i + j
                    out = halves(dot(kk[0], part)) + low[:, j * NS : (j + 1) * NS]
                    out = (out.reshape(SLOTS, 8, NS) * scale[r * 8 : r * 8 + 8][None]).reshape(GROWS, NS)
                    loc[r * GROWS : (r + 1) * GROWS] = split(out)

    def step(k, carry):
        alpha = jnp.where(k == 0, 1.0, 2.0) / span
        beta = jnp.where(k == 0, 0.0, 1.0)
        gather_owned()
        take_faces()
        gather_ghosts()
        apply_cells()
        back = halves(dot(t_gho[...], loc[...]))
        back_send[0] = back[:FACE]
        back_send[1] = back[FACE:]
        for copy in pair(back_send, back_recv, back_sems):
            copy.start()
        for j, (first, last) in enumerate(CHUNK_BLOCKS):
            at = slice(j * FACE, (j + 1) * FACE)
            lanes = slice(CHUNK_AT[j] * ROWS, (CHUNK_AT[j] + last - first) * ROWS)
            added = halves(dot(t_own[:, lanes], loc[first * ROWS : last * ROWS]))
            now = cur[at]
            new = alpha * (added + (pot[at] - centre) * now) - beta * prev[at]
            prev[at] = now
            cur[at] = new
            ext[at] = split(new)
        face_part[...] = halves(dot(pick[...], ext[...]))
        for copy in pair(back_send, back_recv, back_sems):
            copy.wait()
        low, high = received(back_recv)
        extg[:FACE] = split(alpha * low)
        extg[FACE:] = split(alpha * high)
        send_faces(face_part[...] + halves(dot(cross[...], extg[...])))
        for j in range(COUNT // FACE):
            at = slice(j * FACE, (j + 1) * FACE)
            new = cur[at] + halves(dot(pick_t[at], extg[...]))
            cur[at] = new
            ext[at] = split(new)
        return carry

    lax.fori_loop(0, DEG, step, 0)

    share = 1.0 / (total * COUNT)
    corr_sum.start_first(quarters(dot(ext[...], ext[...], ((0,), (0,)))) * share)
    gather_owned()
    take_faces()
    corr_sum.start_second()
    gather_ghosts()
    apply_cells()
    corr_sum.start_third()
    gram = jnp.zeros((2 * NS, 2 * NS), F32)
    for b in range(BLOCKS):
        gram = gram + dot(gath[b], loc[b * ROWS : (b + 1) * ROWS], ((0,), (0,)))
    for j in range(COUNT // FACE):
        at = slice(j * FACE, (j + 1) * FACE)
        gram = gram + dot(ext[at], split(pot[at] * cur[at]), ((0,), (0,)))
    gram_sum.start_first(quarters(gram) * share)
    left[...] = corr_sum.finish()
    right[...] = jnp.where(
        lax.broadcasted_iota(jnp.int32, (NS, NS), 0) == lax.broadcasted_iota(jnp.int32, (NS, NS), 1),
        1.0,
        0.0,
    ).astype(F32)
    for p in range(6):
        factor_panel(p, left, right)
    gram_sum.start_second()
    for p in range(6, NS // 8):
        factor_panel(p, left, right)
    gram_sum.start_third()
    inv = right[...]
    hi = inv.astype(BF16)
    low = (inv - hi.astype(F32)).astype(BF16)
    wide = jnp.concatenate([hi, hi], axis=1)
    narrow = jnp.concatenate([low, jnp.zeros_like(low)], axis=1)
    weights = jnp.concatenate([wide, narrow], axis=0)
    for j in range(COUNT // FACE):
        at = slice(j * FACE, (j + 1) * FACE)
        ortho_ref[at] = halves(dot(ext[at], weights, ((1,), (1,))))
    hgram = gram_sum.finish()
    rows_grid = n_grp // 4
    high = lax.Precision.HIGHEST
    r = grp // 4
    q = lax.rem(grp, 4)
    jump = 8 * rows_grid
    mine = jnp.concatenate(
        [right[pl.ds(pl.multiple_of(jump * t + 8 * r, 8), 8)] for t in range(NS // jump)], axis=0
    )
    other = jnp.concatenate(
        [right[pl.ds(pl.multiple_of(32 * t + 8 * q, 8), 8)] for t in range(NS // 32)], axis=0
    )
    mine = jnp.dot(mine, hgram, precision=high, preferred_element_type=F32)
    tile_ref[...] = lax.dot_general(
        mine, other, (((1,), (1,)), ((), ())), precision=high, preferred_element_type=F32
    )


def whole(n_dom, n_grp, operands):
    piece = NS // n_grp
    rows_grid = n_grp // 4
    vmem = pl.BlockSpec(memory_space=pltpu.VMEM)
    smem = pl.BlockSpec(memory_space=pltpu.SMEM)
    dma = pltpu.SemaphoreType.DMA
    one_sum = [
        pltpu.VMEM((n_grp, piece, NS), F32),
        pltpu.VMEM((n_grp, piece, NS), F32),
        pltpu.VMEM((2, piece, NS), F32),
        pltpu.VMEM((n_dom, piece, NS), F32),
        pltpu.VMEM((n_grp, piece, NS), F32),
        dma((2, n_grp)),
        dma((2, n_dom)),
        dma((2, n_grp)),
    ]
    faces = pltpu.VMEM((2, FACE, NS), F32)
    field = pltpu.VMEM((COUNT, NS), F32)
    return pl.pallas_call(
        functools.partial(filter_kernel, n_dom, n_grp),
        out_shape=(
            jax.ShapeDtypeStruct((COUNT, NS), F32),
            jax.ShapeDtypeStruct((NS // rows_grid, NS // 4), F32),
        ),
        in_specs=[smem] * 3 + [vmem] * 6,
        out_specs=(vmem, vmem),
        scratch_shapes=[
            pltpu.VMEM((BLOCKS, ROWS, WIN), BF16),
            pltpu.VMEM((BLOCKS, ROWS, GHOST), BF16),
            pltpu.VMEM((FACE, CHUNK_ALL * ROWS), BF16),
            pltpu.VMEM((GHOST, BLOCKS * ROWS), BF16),
            pltpu.VMEM((2 * FACE, COUNT), BF16),
            pltpu.VMEM((COUNT, 2 * FACE), BF16),
            pltpu.VMEM((2 * FACE, 2 * FACE), BF16),
            pltpu.VMEM((2, GROWS, GROWS), BF16),
            pltpu.VMEM((BLOCKS, ROWS, 2 * NS), BF16),
            pltpu.VMEM((BLOCKS * ROWS, 2 * NS), BF16),
            pltpu.VMEM((COUNT, 2 * NS), BF16),
            pltpu.VMEM((GHOST, 2 * NS), BF16),
            field,
            field,
            field,
            pltpu.VMEM((2 * NS, NS), F32),
            pltpu.VMEM((2 * FACE, NS), F32),
            faces,
            faces,
            faces,
            faces,
            pltpu.VMEM((NS, NS), F32),
            pltpu.VMEM((NS, NS), F32),
            dma((4,)),
            dma((4,)),
            *one_sum,
            *one_sum,
        ],
        compiler_params=pltpu.CompilerParams(
            collective_id=0, has_side_effects=True, vmem_limit_bytes=62 * 1024 * 1024
        ),
    )(*operands)


def body(
    states,
    potential,
    cell_scale,
    stiffness,
    connect,
    face_nodes,
    node_count,
    filter_cut,
    spectrum_top,
):
    cells = cell_scale.shape[0]
    start = jnp.minimum(jnp.arange(cells, dtype=jnp.int32) // 32, 6) * FACE
    column = jnp.where(
        connect < FACE,
        connect + WIN,
        jnp.where(connect >= FACE + COUNT, connect - FACE - COUNT + WIN + FACE, connect - FACE - start),
    )
    column = jnp.pad(column, ((0, SLOTS - NPC), (0, 0)), constant_values=-1)
    column = column.reshape(SLOTS, BLOCKS, GROUPS, 8).transpose(1, 2, 0, 3).reshape(BLOCKS, ROWS)
    return whole(
        lax.axis_size("dom"),
        lax.axis_size("grp"),
        (
            filter_cut,
            spectrum_top,
            node_count,
            states,
            potential.reshape(COUNT // NS, NS),
            cell_scale.reshape(cells // NS, NS),
            stiffness,
            column,
            face_nodes,
        ),
    )


def solution(mesh):
    placed = (
        P(("dom", "grp"), None),
        P(("dom", "grp")),
        P(("dom", "grp")),
        P(),
        P(None, ("dom", "grp")),
        P(None, ("dom", "grp")),
        P(("dom", "grp")),
        P(),
        P(),
    )
    return jax.shard_map(
        body,
        mesh=mesh,
        in_specs=placed,
        out_specs=(P(("dom", "grp"), None), P("grp", None)),
        check_vma=False,
    )
```

```python
import functools

import jax
import jax.numpy as jnp
from jax import lax
from jax.experimental import pallas as pl
from jax.experimental.pallas import tpu as pltpu
from jax.sharding import PartitionSpec as P

NB = 8
NS = 128
NPC = 27
CELLS = 256
SLOTS = 28
DEG = 4
COUNT = 2048
FACE = 256
BLOCKS = 8
GROUPS = 4
GROWS = SLOTS * 8
ROWS = GROUPS * GROWS
WIN = 2 * FACE
GHOST = 2 * FACE

F32 = jnp.float32
BF16 = jnp.bfloat16
MESH = pl.DeviceIdType.MESH


def dot(a, b, dims=((1,), (0,))):
    return lax.dot_general(a, b, (dims, ((), ())), preferred_element_type=F32)


def split(x):
    hi = x.astype(BF16)
    lo = (x - hi.astype(F32)).astype(BF16)
    return jnp.concatenate([hi, lo], axis=1)


def halves(x):
    return x[:, :NS] + x[:, NS:]


def quarters(x):
    return (x[:NS, :NS] + x[NS:, NS:]) + (x[:NS, NS:] + x[NS:, :NS])


CHUNK_BLOCKS = ((0, 1), (0, 2), (1, 3), (2, 4), (3, 5), (4, 6), (5, 8), (6, 8))
CHUNK_AT = (0, 1, 3, 5, 7, 9, 11, 14)
CHUNK_ALL = 16


class Sum:
    def __init__(self, n_dom, n_grp, dom, grp, refs):
        self.src, self.slots, self.part, self.doms, self.out, self.sems1, self.sems2, self.sems3 = refs
        self.n_dom, self.n_grp, self.dom, self.grp = n_dom, n_grp, dom, grp

    def grp_copy(self, s, src, dst, sems):
        return pltpu.make_async_remote_copy(
            src_ref=src, dst_ref=dst, send_sem=sems.at[0, s], recv_sem=sems.at[1, s],
            device_id=(self.dom, lax.rem(self.grp + s, self.n_grp)), device_id_type=MESH,
        )

    def first(self):
        return [
            self.grp_copy(s, self.src.at[lax.rem(self.grp + s, self.n_grp)], self.slots.at[s], self.sems1)
            for s in range(1, self.n_grp)
        ]

    def second(self):
        return [
            pltpu.make_async_remote_copy(
                src_ref=self.part.at[0], dst_ref=self.doms.at[self.dom],
                send_sem=self.sems2.at[0, s], recv_sem=self.sems2.at[1, s],
                device_id=(lax.rem(self.dom + s, self.n_dom), self.grp), device_id_type=MESH,
            )
            for s in range(1, self.n_dom)
        ]

    def third(self):
        return [
            self.grp_copy(s, self.part.at[1], self.out.at[self.grp], self.sems3)
            for s in range(1, self.n_grp)
        ]

    def start_first(self, value):
        piece = NS // self.n_grp
        for j in range(self.n_grp):
            self.src[j] = value[j * piece : (j + 1) * piece]
        for copy in self.first():
            copy.start()
        self.slots[0] = self.src[self.grp]

    def start_second(self):
        for copy in self.first():
            copy.wait()
        self.part[0] = jnp.sum(self.slots[...], axis=0)
        for copy in self.second():
            copy.start()
        self.doms[self.dom] = self.part[0]

    def start_third(self):
        for copy in self.second():
            copy.wait()
        self.part[1] = jnp.sum(self.doms[...], axis=0)
        for copy in self.third():
            copy.start()
        self.out[self.grp] = self.part[1]

    def finish(self):
        for copy in self.third():
            copy.wait()
        return self.out[...].reshape(NS, NS)


def triple(x):
    hi = x.astype(BF16).astype(F32)
    rest = x - hi
    mid = rest.astype(BF16).astype(F32)
    return hi, mid, rest - mid


def factor_panel(p, left_ref, right_ref, inv_ref):
    sub = lax.broadcasted_iota(jnp.int32, (8, NS), 0)
    a = left_ref[:8]
    m = right_ref[:8]
    cols = [jnp.broadcast_to(a[:, k : k + 1], (8, NS)) for k in range(8)]
    pivots = jnp.ones((8, NS), F32)
    for j in range(8):
        at = [None] * j + [jnp.broadcast_to(cols[k][j : j + 1], (8, NS)) for k in range(j, 8)]
        mult = jnp.where(sub > j, cols[j] * (1.0 / at[j]), 0.0)
        for k in range(j + 1, 8):
            cols[k] = cols[k] - mult * at[k]
        a, m = (
            a - mult * jnp.broadcast_to(a[j : j + 1], (8, NS)),
            m - mult * jnp.broadcast_to(m[j : j + 1], (8, NS)),
        )
        pivots = jnp.where(sub == j, at[j], pivots)
    scale = 1.0 / jnp.sqrt(pivots)
    a, m = a * scale, m * scale
    inv_ref[pl.ds(pl.multiple_of(8 * p, 8), 8)] = m
    a = jnp.concatenate([a[:, 8:], jnp.zeros((8, 8), F32)], axis=1)
    hi, mid, low = triple(a)
    mhi, mmid, mlow = triple(m)
    one = jnp.concatenate([hi, hi, mid, hi, low, mid], axis=0).astype(BF16)
    two = jnp.concatenate([hi, mid, hi, low, hi, mid], axis=0)
    two_m = jnp.concatenate([mhi, mmid, mhi, mlow, mhi, mmid], axis=0)
    two = jnp.concatenate([two, two_m], axis=1).astype(BF16)
    both = dot(one, two, ((0,), (0,)))[: NS - 8]
    rest = left_ref[8:]
    rest = jnp.concatenate([rest[:, 8:], jnp.zeros((NS - 8, 8), F32)], axis=1)
    left_ref[: NS - 8] = rest - both[:, :NS]
    right_ref[: NS - 8] = right_ref[8:] - both[:, NS:]


def filter_kernel(
    n_dom,
    n_grp,
    cut_ref,
    top_ref,
    live_ref,
    states_ref,
    pot_ref,
    scale_ref,
    kmat_ref,
    conn_ref,
    face_ref,
    ortho_ref,
    tile_ref,
    g_own,
    g_gho,
    t_own,
    t_gho,
    pick,
    pick_t,
    cross,
    kk,
    gath,
    loc,
    ext,
    extg,
    extr,
    a_far,
    cur,
    prev,
    pot,
    scale,
    face_part,
    face_send,
    face_recv,
    back_send,
    back_recv,
    left,
    right,
    inverse,
    conn_col,
    conn_row,
    far_part,
    gram_acc,
    face_sems,
    back_sems,
    *sums,
):
    dom = lax.axis_index("dom")
    grp = lax.axis_index("grp")
    total = n_dom * n_grp
    me = dom * n_grp + grp
    up = lax.rem(me + 1, total)
    down = lax.rem(me + total - 1, total)
    even = lax.rem(grp, 2) == 0
    near_at = jnp.where(even, up, down)
    far_at = jnp.where(even, down, up)
    ids = [(at // n_grp, lax.rem(at, n_grp)) for at in (near_at, far_at)]
    edge = jnp.logical_or(me == 0, me == total - 1)
    partners = list(ids)
    partners += [(dom, lax.rem(grp + s, n_grp)) for s in range(1, n_grp)]
    partners += [(lax.rem(dom + s, n_dom), grp) for s in range(1, n_dom)]
    barrier = pltpu.get_barrier_semaphore()
    for device in partners:
        pl.semaphore_signal(barrier, inc=1, device_id=device, device_id_type=MESH)
    corr_sum = Sum(n_dom, n_grp, dom, grp, sums[: len(sums) // 2])
    gram_sum = Sum(n_dom, n_grp, dom, grp, sums[len(sums) // 2 :])

    def swap(side, send, recv, sems):
        return pltpu.make_async_remote_copy(
            src_ref=send.at[side], dst_ref=recv.at[side],
            send_sem=sems.at[side, 0], recv_sem=sems.at[side, 1],
            device_id=ids[side], device_id_type=MESH,
        )

    def send_faces(values):
        for side in (1, 0):
            face_send[side] = values[side * FACE : (side + 1) * FACE]
            swap(side, face_send, face_recv, face_sems).start()

    def take_face(side):
        swap(side, face_send, face_recv, face_sems).wait()
        value = face_recv[side] if side == 0 else jnp.where(edge, 0.0, face_recv[side])
        extg[side * FACE : (side + 1) * FACE] = split(value)

    def send_back(side, value):
        back_send[side] = value
        swap(side, back_send, back_recv, back_sems).start()

    def take_back(side, alpha):
        swap(side, back_send, back_recv, back_sems).wait()
        value = back_recv[side] if side == 0 else jnp.where(edge, 0.0, back_recv[side])
        extr[side * FACE : (side + 1) * FACE] = split(alpha * value)

    live = live_ref[0]
    lower, upper = face_ref[0:1], face_ref[1:2]
    faces = [jnp.where(even, upper, lower), jnp.where(even, lower, upper)]
    face_rows = jnp.concatenate(
        [faces[0][:, :NS], faces[0][:, NS:], faces[1][:, :NS], faces[1][:, NS:]], axis=0
    ).astype(F32)
    stacked = jnp.concatenate(
        [pot_ref[...], scale_ref[...], face_rows, jnp.zeros((2, NS), F32)], axis=0
    )
    columns = stacked.T
    wants = jnp.concatenate([columns[:, c : c + 1] for c in (18, 19, 20, 21)], axis=0).astype(jnp.int32)
    wants = jnp.broadcast_to(wants, (2 * FACE, NS))

    def first_field(i, carry):
        start = pl.multiple_of(i * NS, NS)
        at = pl.ds(start, NS)
        node = lax.broadcasted_iota(jnp.int32, (NS, NS), 0) + start
        value = jnp.where(node < live, states_ref[at], 0.0)
        cur[at] = value
        prev[at] = jnp.zeros((NS, NS), F32)
        ext[at] = split(value)
        lane = lax.broadcasted_iota(jnp.int32, (2 * FACE, NS), 1) + start
        pick[:, at] = jnp.where(wants == lane, 1.0, 0.0).astype(BF16)
        return carry

    lax.fori_loop(0, COUNT // NS, first_field, 0)
    face_part[...] = halves(dot(pick[...], ext[...]))

    raw = jnp.concatenate([conn_ref[...], jnp.full((32 - NPC, CELLS), -1, jnp.int32)], axis=0)
    cell = lax.broadcasted_iota(jnp.int32, (32, CELLS), 1)
    start = jnp.minimum(cell // 32, 6) * FACE
    low_at = WIN + jnp.where(even, FACE, 0)
    high_at = WIN + jnp.where(even, 0, FACE)
    column = jnp.where(
        raw < FACE,
        raw + low_at,
        jnp.where(raw >= FACE + COUNT, raw - (FACE + COUNT) + high_at, raw - FACE - start),
    )
    column = jnp.where(raw < 0, -1, column)
    by_cell = column.astype(F32).T
    lane = lax.broadcasted_iota(jnp.int32, (ROWS, NS), 1)
    packed = jnp.zeros((ROWS, NS), F32)
    for b in range(BLOCKS):
        pieces = []
        for r in range(b * GROUPS, (b + 1) * GROUPS):
            pieces += [by_cell[8 * r : 8 * r + 8, a : a + 1] for a in range(SLOTS)]
        col = jnp.concatenate([jnp.broadcast_to(piece, (8, NS)) for piece in pieces], axis=0)
        conn_col[b] = col.astype(jnp.int32)
        packed = jnp.where(lane == b, col, packed)
    conn_row[...] = packed.T[:BLOCKS].astype(jnp.int32)

    pl.semaphore_wait(barrier, len(partners))
    send_faces(face_part[...])

    def build(b, carry):
        col = conn_col[b]
        col = jnp.concatenate([col] * (WIN // NS), axis=1)
        lane = lax.broadcasted_iota(jnp.int32, (ROWS, WIN), 1)
        g_own[b] = jnp.where(col == lane, 1.0, 0.0).astype(BF16)
        g_gho[b] = jnp.where(col == lane + WIN, 1.0, 0.0).astype(BF16)
        row = conn_row[pl.ds(b, 1)]
        sub = lax.broadcasted_iota(jnp.int32, (WIN, ROWS), 0)
        gho = jnp.where(row == sub + WIN, 1.0, 0.0).astype(BF16)
        t_gho[:, pl.ds(pl.multiple_of(b * ROWS, NS), ROWS)] = gho
        own = jnp.where(row == sub, 1.0, 0.0).astype(BF16)
        at = jnp.where(b < 7, 2 * b, 13)
        t_own[:, pl.ds(pl.multiple_of(at * ROWS, NS), ROWS)] = own[:FACE]
        at = jnp.where(b < 6, 2 * b + 1, b + 8)
        t_own[:, pl.ds(pl.multiple_of(at * ROWS, NS), ROWS)] = own[FACE:]
        return carry

    lax.fori_loop(0, BLOCKS, build, 0)

    def build_pick(i, carry):
        start = pl.multiple_of(i * NS, NS)
        sub = lax.broadcasted_iota(jnp.int32, (NS, FACE), 0) + start
        for side in range(2):
            value = jnp.where(faces[side] == sub, 1.0, 0.0).astype(BF16)
            pick_t[pl.ds(start, NS), side * FACE : (side + 1) * FACE] = value
        return carry

    lax.fori_loop(0, COUNT // NS, build_pick, 0)
    cross[...] = dot(pick[...], pick_t[...]).astype(BF16)
    spread = (
        lax.broadcasted_iota(jnp.int32, (GROWS, NPC), 0) // 8
        == lax.broadcasted_iota(jnp.int32, (GROWS, NPC), 1)
    )
    spread = jnp.where(spread, 1.0, 0.0).astype(F32)
    wide = lax.dot_general(
        spread, kmat_ref[...], (((1,), (0,)), ((), ())),
        precision=lax.Precision.HIGHEST, preferred_element_type=F32,
    )
    wide = lax.dot_general(
        wide, spread, (((1,), (1,)), ((), ())),
        precision=lax.Precision.HIGHEST, preferred_element_type=F32,
    )
    same = lax.rem(lax.broadcasted_iota(jnp.int32, (GROWS, GROWS), 0), 8) == lax.rem(
        lax.broadcasted_iota(jnp.int32, (GROWS, GROWS), 1), 8
    )
    wide = jnp.where(same, wide, 0.0)
    kk[0] = wide.astype(BF16)
    kk[1] = (wide - wide.astype(BF16).astype(F32)).astype(BF16)
    for i in range(COUNT // NS):
        pot[i * NS : (i + 1) * NS] = jnp.broadcast_to(columns[:, i : i + 1], (NS, NS))
    for i in range(2):
        cell = lax.broadcasted_iota(jnp.int32, (NS, NS), 0) + i * NS
        value = jnp.broadcast_to(columns[:, 16 + i : 17 + i], (NS, NS))
        scale[i * NS : (i + 1) * NS] = jnp.where(8 * cell + 8 <= live, value, 0.0)
    span = (top_ref[0] - cut_ref[0]) * 0.5
    centre = (top_ref[0] + cut_ref[0]) * 0.5

    def gather_owned():
        for b in range(BLOCKS):
            at = min(b, 6) * FACE
            gath[b] = dot(g_own[b], ext[at : at + WIN]).astype(BF16)

    def gather_side(side):
        at = slice(side * FACE, (side + 1) * FACE)
        for b in range(BLOCKS):
            gath[b] = gath[b] + dot(g_gho[b, :, at], extg[at]).astype(BF16)

    def scatter_side(side):
        return halves(dot(t_gho[side * FACE : (side + 1) * FACE], loc[...]))

    def far_far():
        values = extg[FACE:]
        return halves(dot(a_far[0], values)) + dot(a_far[1], values[:, :NS])

    def apply_cells():
        for b in range(BLOCKS):
            for i in range(0, GROUPS, 2):
                one = gath[b, i * GROWS : (i + 1) * GROWS]
                two = gath[b, (i + 1) * GROWS : (i + 2) * GROWS]
                low = dot(kk[1], jnp.concatenate([one[:, :NS], two[:, :NS]], axis=1))
                for j, part in enumerate((one, two)):
                    r = b * GROUPS + i + j
                    out = halves(dot(kk[0], part)) + low[:, j * NS : (j + 1) * NS]
                    out = (out.reshape(SLOTS, 8, NS) * scale[r * 8 : r * 8 + 8][None]).reshape(GROWS, NS)
                    loc[r * GROWS : (r + 1) * GROWS] = split(out)

    def build_far():
        def far_block(h, carry):
            for t in range(2):
                b = 2 * h + t
                for i in range(GROUPS):
                    part = g_gho[b, i * GROWS : (i + 1) * GROWS, FACE:]
                    out = dot(kk[0], part) + dot(kk[1], part)
                    by = scale[pl.ds(pl.multiple_of(b * 8 * GROUPS + 8 * i, 8), 8)]
                    by = jnp.concatenate([by, by], axis=1)
                    out = (out.reshape(SLOTS, 8, FACE) * by[None]).reshape(GROWS, FACE)
                    out_hi = out.astype(BF16)
                    gath[b, i * GROWS : (i + 1) * GROWS] = out_hi
                    loc[pl.ds(pl.multiple_of(b * ROWS + i * GROWS, 16), GROWS)] = (
                        out - out_hi.astype(F32)
                    ).astype(BF16)
            return carry

        lax.fori_loop(0, BLOCKS // 2, far_block, 0)
        out = dot(t_gho[FACE:], gath[...].reshape(BLOCKS * ROWS, FACE)) + dot(t_gho[FACE:], loc[...])
        a_far[0] = out.astype(BF16)
        a_far[1] = (out - out.astype(BF16).astype(F32)).astype(BF16)

    def step(k, carry):
        alpha = jnp.where(k == 0, 1.0, 2.0) / span
        beta = jnp.where(k == 0, 0.0, 1.0)
        @pl.when(k == DEG)
        def _():
            corr_sum.start_first(quarters(dot(ext[...], ext[...], ((0,), (0,)))) * share)

        gather_owned()
        take_face(0)
        gather_side(0)

        @pl.when(k == 0)
        def _():
            take_face(1)
            gather_side(1)

        apply_cells()
        far_part[...] = scatter_side(1)

        @pl.when(k < DEG)
        def _():
            @pl.when(k == 0)
            def _():
                send_back(1, far_part[...])

            @pl.when(k > 0)
            def _():
                take_face(1)
                send_back(1, far_part[...] + far_far())
                gather_side(1)
                apply_cells()

            send_back(0, scatter_side(0))
            for j, (first, last) in enumerate(CHUNK_BLOCKS):
                at = slice(j * FACE, (j + 1) * FACE)
                lanes = slice(CHUNK_AT[j] * ROWS, (CHUNK_AT[j] + last - first) * ROWS)
                added = halves(dot(t_own[:, lanes], loc[first * ROWS : last * ROWS]))
                now = cur[at]
                new = alpha * (added + (pot[at] - centre) * now) - beta * prev[at]
                prev[at] = now
                cur[at] = new
                ext[at] = split(new)
            face_part[...] = halves(dot(pick[...], ext[...]))

            @pl.when(k == 0)
            def _():
                build_far()

            take_back(0, alpha)
            take_back(1, alpha)
            send_faces(face_part[...] + halves(dot(cross[...], extr[...])))
            for j in range(COUNT // FACE):
                at = slice(j * FACE, (j + 1) * FACE)
                new = cur[at] + halves(dot(pick_t[at], extr[...]))
                cur[at] = new
                ext[at] = split(new)

        return carry

    share = 1.0 / (total * COUNT)
    lax.fori_loop(0, DEG + 1, step, 0)

    corr_sum.start_second()
    gram_acc[...] = jnp.zeros((2 * NS, 2 * NS), F32)

    def gram_block(b, carry):
        rows = loc[pl.ds(pl.multiple_of(b * ROWS, NS), ROWS)]
        at = pl.ds(pl.multiple_of(b * FACE, FACE), FACE)
        gram_acc[...] += dot(gath[b], rows, ((0,), (0,))) + dot(
            ext[at], split(pot[at] * cur[at]), ((0,), (0,))
        )
        return carry

    lax.fori_loop(0, BLOCKS, gram_block, 0)
    take_face(1)
    mixed = quarters(dot(extg[FACE:], split(far_part[...] + 0.5 * far_far()), ((0,), (0,))))
    gram_sum.start_first((quarters(gram_acc[...]) + (mixed + mixed.T)) * share)
    corr_sum.start_third()
    gram_sum.start_second()
    left[...] = corr_sum.finish()
    right[...] = jnp.where(
        lax.broadcasted_iota(jnp.int32, (NS, NS), 0) == lax.broadcasted_iota(jnp.int32, (NS, NS), 1),
        1.0,
        0.0,
    ).astype(F32)
    def panel(p, carry):
        factor_panel(p, left, right, inverse)
        return carry

    lax.fori_loop(0, NS // 16, panel, 0)
    gram_sum.start_third()
    lax.fori_loop(NS // 16, NS // 8, panel, 0)
    inv = inverse[...]
    hi = inv.astype(BF16)
    low = (inv - hi.astype(F32)).astype(BF16)
    wide = jnp.concatenate([hi, hi], axis=1)
    narrow = jnp.concatenate([low, jnp.zeros_like(low)], axis=1)
    weights = jnp.concatenate([wide, narrow], axis=0)
    for j in range(COUNT // FACE):
        at = slice(j * FACE, (j + 1) * FACE)
        ortho_ref[at] = halves(dot(ext[at], weights, ((1,), (1,))))
    hgram = gram_sum.finish()
    rows_grid = n_grp // 4
    high = lax.Precision.HIGHEST
    r = grp // 4
    q = lax.rem(grp, 4)
    jump = 8 * rows_grid
    mine = jnp.concatenate(
        [inverse[pl.ds(pl.multiple_of(jump * t + 8 * r, 8), 8)] for t in range(NS // jump)], axis=0
    )
    other = jnp.concatenate(
        [inverse[pl.ds(pl.multiple_of(32 * t + 8 * q, 8), 8)] for t in range(NS // 32)], axis=0
    )
    mine = jnp.dot(mine, hgram, precision=high, preferred_element_type=F32)
    tile_ref[...] = lax.dot_general(
        mine, other, (((1,), (1,)), ((), ())), precision=high, preferred_element_type=F32
    )


def whole(n_dom, n_grp, operands):
    piece = NS // n_grp
    rows_grid = n_grp // 4
    vmem = pl.BlockSpec(memory_space=pltpu.VMEM)
    smem = pl.BlockSpec(memory_space=pltpu.SMEM)
    dma = pltpu.SemaphoreType.DMA
    one_sum = [
        pltpu.VMEM((n_grp, piece, NS), F32),
        pltpu.VMEM((n_grp, piece, NS), F32),
        pltpu.VMEM((2, piece, NS), F32),
        pltpu.VMEM((n_dom, piece, NS), F32),
        pltpu.VMEM((n_grp, piece, NS), F32),
        dma((2, n_grp)),
        dma((2, n_dom)),
        dma((2, n_grp)),
    ]
    faces = pltpu.VMEM((2, FACE, NS), F32)
    field = pltpu.VMEM((COUNT, NS), F32)
    return pl.pallas_call(
        functools.partial(filter_kernel, n_dom, n_grp),
        out_shape=(
            jax.ShapeDtypeStruct((COUNT, NS), F32),
            jax.ShapeDtypeStruct((NS // rows_grid, NS // 4), F32),
        ),
        in_specs=[smem] * 3 + [vmem] * 6,
        out_specs=(vmem, vmem),
        scratch_shapes=[
            pltpu.VMEM((BLOCKS, ROWS, WIN), BF16),
            pltpu.VMEM((BLOCKS, ROWS, GHOST), BF16),
            pltpu.VMEM((FACE, CHUNK_ALL * ROWS), BF16),
            pltpu.VMEM((GHOST, BLOCKS * ROWS), BF16),
            pltpu.VMEM((2 * FACE, COUNT), BF16),
            pltpu.VMEM((COUNT, 2 * FACE), BF16),
            pltpu.VMEM((2 * FACE, 2 * FACE), BF16),
            pltpu.VMEM((2, GROWS, GROWS), BF16),
            pltpu.VMEM((BLOCKS, ROWS, 2 * NS), BF16),
            pltpu.VMEM((BLOCKS * ROWS, 2 * NS), BF16),
            pltpu.VMEM((COUNT, 2 * NS), BF16),
            pltpu.VMEM((GHOST, 2 * NS), BF16),
            pltpu.VMEM((GHOST, 2 * NS), BF16),
            pltpu.VMEM((2, FACE, FACE), BF16),
            field,
            field,
            field,
            pltpu.VMEM((2 * NS, NS), F32),
            pltpu.VMEM((2 * FACE, NS), F32),
            faces,
            faces,
            faces,
            faces,
            pltpu.VMEM((NS, NS), F32),
            pltpu.VMEM((NS, NS), F32),
            pltpu.VMEM((NS, NS), F32),
            pltpu.VMEM((BLOCKS, ROWS, NS), jnp.int32),
            pltpu.VMEM((BLOCKS, ROWS), jnp.int32),
            pltpu.VMEM((FACE, NS), F32),
            pltpu.VMEM((2 * NS, 2 * NS), F32),
            dma((2, 2)),
            dma((2, 2)),
            *one_sum,
            *one_sum,
        ],
        compiler_params=pltpu.CompilerParams(
            collective_id=0, has_side_effects=True, vmem_limit_bytes=62 * 1024 * 1024
        ),
    )(*operands)


def body(
    states,
    potential,
    cell_scale,
    stiffness,
    connect,
    face_nodes,
    node_count,
    filter_cut,
    spectrum_top,
):
    return whole(
        lax.axis_size("dom"),
        lax.axis_size("grp"),
        (
            filter_cut,
            spectrum_top,
            node_count,
            states,
            potential.reshape(COUNT // NS, NS),
            cell_scale.reshape(CELLS // NS, NS),
            stiffness,
            connect,
            face_nodes,
        ),
    )


def solution(mesh):
    placed = (
        P(("dom", "grp"), None),
        P(("dom", "grp")),
        P(("dom", "grp")),
        P(),
        P(None, ("dom", "grp")),
        P(None, ("dom", "grp")),
        P(("dom", "grp")),
        P(),
        P(),
    )
    return jax.shard_map(
        body,
        mesh=mesh,
        in_specs=placed,
        out_specs=(P(("dom", "grp"), None), P("grp", None)),
        check_vma=False,
    )
```

```python
import functools

import jax
import jax.numpy as jnp
from jax import lax
from jax.experimental import pallas as pl
from jax.experimental.pallas import tpu as pltpu
from jax.sharding import PartitionSpec as P

NB = 8
NS = 128
NPC = 27
CELLS = 256
SLOTS = 28
DEG = 4
COUNT = 2048
FACE = 256
BLOCKS = 8
GROUPS = 4
GROWS = SLOTS * 8
ROWS = GROUPS * GROWS
WIN = 2 * FACE
GHOST = 2 * FACE

F32 = jnp.float32
BF16 = jnp.bfloat16
MESH = pl.DeviceIdType.MESH


def dot(a, b, dims=((1,), (0,))):
    return lax.dot_general(a, b, (dims, ((), ())), preferred_element_type=F32)


def split(x):
    hi = x.astype(BF16)
    lo = (x - hi.astype(F32)).astype(BF16)
    return jnp.concatenate([hi, lo], axis=1)


def halves(x):
    return x[:, :NS] + x[:, NS:]


def quarters(x):
    return (x[:NS, :NS] + x[NS:, NS:]) + (x[:NS, NS:] + x[NS:, :NS])


CHUNK_BLOCKS = ((0, 1), (0, 2), (1, 3), (2, 4), (3, 5), (4, 6), (5, 8), (6, 8))
CHUNK_AT = (0, 1, 3, 5, 7, 9, 11, 14)
CHUNK_ALL = 16


class Sum:
    def __init__(self, n_dom, n_grp, dom, grp, refs):
        self.src, self.slots, self.part, self.sums, self.out, self.sems1, self.sems2, self.sems3 = refs
        self.n_in = n_grp // 2
        self.n_out = 2 * n_dom
        self.inner = lax.rem(grp, self.n_in)
        self.outer = dom * 2 + grp // self.n_in

    def device(self, outer, inner):
        return (outer // 2, lax.rem(outer, 2) * self.n_in + inner)

    def in_partner(self, s):
        return lax.rem(self.inner + s, self.n_in)

    def partners(self):
        found = [self.device(self.outer, self.in_partner(s)) for s in range(1, self.n_in)]
        return found + [
            self.device(lax.rem(self.outer + s, self.n_out), self.inner) for s in range(1, self.n_out)
        ]

    def in_copy(self, s, src, dst, sems):
        return pltpu.make_async_remote_copy(
            src_ref=src, dst_ref=dst, send_sem=sems.at[0, s], recv_sem=sems.at[1, s],
            device_id=self.device(self.outer, self.in_partner(s)), device_id_type=MESH,
        )

    def first(self):
        return [
            self.in_copy(s, self.src.at[self.in_partner(s)], self.slots.at[s], self.sems1)
            for s in range(1, self.n_in)
        ]

    def second(self):
        return [
            pltpu.make_async_remote_copy(
                src_ref=self.part.at[0], dst_ref=self.sums.at[self.outer],
                send_sem=self.sems2.at[0, s], recv_sem=self.sems2.at[1, s],
                device_id=self.device(lax.rem(self.outer + s, self.n_out), self.inner),
                device_id_type=MESH,
            )
            for s in range(1, self.n_out)
        ]

    def third(self):
        return [
            self.in_copy(s, self.part.at[1], self.out.at[self.inner], self.sems3)
            for s in range(1, self.n_in)
        ]

    def start_first(self, value):
        piece = NS // self.n_in
        for j in range(self.n_in):
            self.src[j] = value[j * piece : (j + 1) * piece]
        for copy in self.first():
            copy.start()
        self.slots[0] = self.src[self.inner]

    def start_second(self):
        for copy in self.first():
            copy.wait()
        self.part[0] = jnp.sum(self.slots[...], axis=0)
        for copy in self.second():
            copy.start()
        self.sums[self.outer] = self.part[0]

    def start_third(self):
        for copy in self.second():
            copy.wait()
        self.part[1] = jnp.sum(self.sums[...], axis=0)
        for copy in self.third():
            copy.start()
        self.out[self.inner] = self.part[1]

    def finish(self):
        for copy in self.third():
            copy.wait()
        return self.out[...].reshape(NS, NS)


def triple(x):
    hi = x.astype(BF16).astype(F32)
    rest = x - hi
    mid = rest.astype(BF16).astype(F32)
    return hi, mid, rest - mid


def factor_panel(p, left_ref, right_ref, inv_ref):
    sub = lax.broadcasted_iota(jnp.int32, (8, NS), 0)
    a = left_ref[:8]
    m = right_ref[:8]
    cols = [jnp.broadcast_to(a[:, k : k + 1], (8, NS)) for k in range(8)]
    pivots = jnp.ones((8, NS), F32)
    for j in range(8):
        at = [None] * j + [jnp.broadcast_to(cols[k][j : j + 1], (8, NS)) for k in range(j, 8)]
        mult = jnp.where(sub > j, cols[j] * (1.0 / at[j]), 0.0)
        for k in range(j + 1, 8):
            cols[k] = cols[k] - mult * at[k]
        a, m = (
            a - mult * jnp.broadcast_to(a[j : j + 1], (8, NS)),
            m - mult * jnp.broadcast_to(m[j : j + 1], (8, NS)),
        )
        pivots = jnp.where(sub == j, at[j], pivots)
    scale = 1.0 / jnp.sqrt(pivots)
    a, m = a * scale, m * scale
    inv_ref[pl.ds(pl.multiple_of(8 * p, 8), 8)] = m
    a = jnp.concatenate([a[:, 8:], jnp.zeros((8, 8), F32)], axis=1)
    hi, mid, low = triple(a)
    mhi, mmid, mlow = triple(m)
    one = jnp.concatenate([hi, hi, mid, hi, low, mid], axis=0).astype(BF16)
    two = jnp.concatenate([hi, mid, hi, low, hi, mid], axis=0)
    two_m = jnp.concatenate([mhi, mmid, mhi, mlow, mhi, mmid], axis=0)
    two = jnp.concatenate([two, two_m], axis=1).astype(BF16)
    both = dot(one, two, ((0,), (0,)))[: NS - 8]
    rest = left_ref[8:]
    rest = jnp.concatenate([rest[:, 8:], jnp.zeros((NS - 8, 8), F32)], axis=1)
    left_ref[: NS - 8] = rest - both[:, :NS]
    right_ref[: NS - 8] = right_ref[8:] - both[:, NS:]


def filter_kernel(
    n_dom,
    n_grp,
    cut_ref,
    top_ref,
    live_ref,
    states_ref,
    pot_ref,
    scale_ref,
    kmat_ref,
    conn_ref,
    face_ref,
    ortho_ref,
    tile_ref,
    g_own,
    g_gho,
    t_own,
    t_gho,
    pick,
    pick_t,
    cross,
    kk,
    gath,
    loc,
    ext,
    extg,
    extr,
    a_far,
    cur,
    prev,
    pot,
    scale,
    face_part,
    face_send,
    face_recv,
    back_send,
    back_recv,
    left,
    right,
    inverse,
    conn_col,
    conn_row,
    far_part,
    gram_acc,
    face_sems,
    back_sems,
    states_sem,
    *sums,
):
    dom = lax.axis_index("dom")
    grp = lax.axis_index("grp")
    total = n_dom * n_grp
    me = dom * n_grp + grp
    up = lax.rem(me + 1, total)
    down = lax.rem(me + total - 1, total)
    even = lax.rem(grp, 2) == 0
    near_at = jnp.where(even, up, down)
    far_at = jnp.where(even, down, up)
    ids = [(at // n_grp, lax.rem(at, n_grp)) for at in (near_at, far_at)]
    edge = jnp.logical_or(me == 0, me == total - 1)
    partners = list(ids)
    corr_sum = Sum(n_dom, n_grp, dom, grp, sums[: len(sums) // 2])
    gram_sum = Sum(n_dom, n_grp, dom, grp, sums[len(sums) // 2 :])
    partners += corr_sum.partners()
    states_copy = pltpu.make_async_copy(states_ref, cur, states_sem)
    states_copy.start()
    barrier = pltpu.get_barrier_semaphore()
    for device in partners:
        pl.semaphore_signal(barrier, inc=1, device_id=device, device_id_type=MESH)

    def swap(side, send, recv, sems):
        return pltpu.make_async_remote_copy(
            src_ref=send.at[side], dst_ref=recv.at[side],
            send_sem=sems.at[side, 0], recv_sem=sems.at[side, 1],
            device_id=ids[side], device_id_type=MESH,
        )

    def send_faces(values):
        for side in (1, 0):
            face_send[side] = values[side * FACE : (side + 1) * FACE]
            swap(side, face_send, face_recv, face_sems).start()

    def take_face(side):
        swap(side, face_send, face_recv, face_sems).wait()
        value = face_recv[side] if side == 0 else jnp.where(edge, 0.0, face_recv[side])
        extg[side * FACE : (side + 1) * FACE] = split(value)

    def send_back(side, value):
        back_send[side] = value
        swap(side, back_send, back_recv, back_sems).start()

    def take_back(side, alpha):
        swap(side, back_send, back_recv, back_sems).wait()
        value = back_recv[side] if side == 0 else jnp.where(edge, 0.0, back_recv[side])
        extr[side * FACE : (side + 1) * FACE] = split(alpha * value)

    live = live_ref[0]
    lower, upper = face_ref[0:1], face_ref[1:2]
    faces = [jnp.where(even, upper, lower), jnp.where(even, lower, upper)]
    face_rows = jnp.concatenate(
        [faces[0][:, :NS], faces[0][:, NS:], faces[1][:, :NS], faces[1][:, NS:]], axis=0
    ).astype(F32)
    stacked = jnp.concatenate(
        [pot_ref[...], scale_ref[...], face_rows, jnp.zeros((2, NS), F32)], axis=0
    )
    columns = stacked.T
    wants = jnp.concatenate([columns[:, c : c + 1] for c in (18, 19, 20, 21)], axis=0).astype(jnp.int32)
    wants = jnp.broadcast_to(wants, (2 * FACE, NS))

    def first_field(i, carry):
        start = pl.multiple_of(i * NS, NS)
        at = pl.ds(start, NS)
        node = lax.broadcasted_iota(jnp.int32, (NS, NS), 0) + start
        value = jnp.where(node < live, cur[at], 0.0)
        cur[at] = value
        prev[at] = jnp.zeros((NS, NS), F32)
        ext[at] = split(value)
        lane = lax.broadcasted_iota(jnp.int32, (2 * FACE, NS), 1) + start
        pick[:, at] = jnp.where(wants == lane, 1.0, 0.0).astype(BF16)
        return carry

    states_copy.wait()
    lax.fori_loop(0, COUNT // NS, first_field, 0)
    face_part[...] = halves(dot(pick[...], ext[...]))

    raw = jnp.concatenate([conn_ref[...], jnp.full((32 - NPC, CELLS), -1, jnp.int32)], axis=0)
    cell = lax.broadcasted_iota(jnp.int32, (32, CELLS), 1)
    start = jnp.minimum(cell // 32, 6) * FACE
    low_at = WIN + jnp.where(even, FACE, 0)
    high_at = WIN + jnp.where(even, 0, FACE)
    column = jnp.where(
        raw < FACE,
        raw + low_at,
        jnp.where(raw >= FACE + COUNT, raw - (FACE + COUNT) + high_at, raw - FACE - start),
    )
    column = jnp.where(raw < 0, -1, column)
    by_cell = column.astype(F32).T
    lane = lax.broadcasted_iota(jnp.int32, (ROWS, NS), 1)
    packed = jnp.zeros((ROWS, NS), F32)
    for b in range(BLOCKS):
        pieces = []
        for r in range(b * GROUPS, (b + 1) * GROUPS):
            pieces += [by_cell[8 * r : 8 * r + 8, a : a + 1] for a in range(SLOTS)]
        col = jnp.concatenate([jnp.broadcast_to(piece, (8, NS)) for piece in pieces], axis=0)
        conn_col[b] = col.astype(jnp.int32)
        packed = jnp.where(lane == b, col, packed)
    conn_row[...] = packed.T[:BLOCKS].astype(jnp.int32)

    pl.semaphore_wait(barrier, len(partners))
    send_faces(face_part[...])

    def build(b, carry):
        col = conn_col[b]
        col = jnp.concatenate([col] * (WIN // NS), axis=1)
        lane = lax.broadcasted_iota(jnp.int32, (ROWS, WIN), 1)
        g_own[b] = jnp.where(col == lane, 1.0, 0.0).astype(BF16)
        g_gho[b] = jnp.where(col == lane + WIN, 1.0, 0.0).astype(BF16)
        row = conn_row[pl.ds(b, 1)]
        sub = lax.broadcasted_iota(jnp.int32, (WIN, ROWS), 0)
        gho = jnp.where(row == sub + WIN, 1.0, 0.0).astype(BF16)
        t_gho[:, pl.ds(pl.multiple_of(b * ROWS, NS), ROWS)] = gho
        own = jnp.where(row == sub, 1.0, 0.0).astype(BF16)
        at = jnp.where(b < 7, 2 * b, 13)
        t_own[:, pl.ds(pl.multiple_of(at * ROWS, NS), ROWS)] = own[:FACE]
        at = jnp.where(b < 6, 2 * b + 1, b + 8)
        t_own[:, pl.ds(pl.multiple_of(at * ROWS, NS), ROWS)] = own[FACE:]
        return carry

    lax.fori_loop(0, BLOCKS, build, 0)

    def build_pick(i, carry):
        start = pl.multiple_of(i * NS, NS)
        sub = lax.broadcasted_iota(jnp.int32, (NS, FACE), 0) + start
        for side in range(2):
            value = jnp.where(faces[side] == sub, 1.0, 0.0).astype(BF16)
            pick_t[pl.ds(start, NS), side * FACE : (side + 1) * FACE] = value
        return carry

    lax.fori_loop(0, COUNT // NS, build_pick, 0)
    for side in range(2):
        row = jnp.broadcast_to(faces[side], (2 * FACE, FACE))
        want = jnp.concatenate([wants, wants], axis=1)
        cross[:, side * FACE : (side + 1) * FACE] = jnp.where(want == row, 1.0, 0.0).astype(BF16)
    spread = (
        lax.broadcasted_iota(jnp.int32, (GROWS, NPC), 0) // 8
        == lax.broadcasted_iota(jnp.int32, (GROWS, NPC), 1)
    )
    spread = jnp.where(spread, 1.0, 0.0).astype(F32)
    wide = lax.dot_general(
        spread, kmat_ref[...], (((1,), (0,)), ((), ())),
        precision=lax.Precision.HIGHEST, preferred_element_type=F32,
    )
    wide = lax.dot_general(
        wide, spread, (((1,), (1,)), ((), ())),
        precision=lax.Precision.HIGHEST, preferred_element_type=F32,
    )
    same = lax.rem(lax.broadcasted_iota(jnp.int32, (GROWS, GROWS), 0), 8) == lax.rem(
        lax.broadcasted_iota(jnp.int32, (GROWS, GROWS), 1), 8
    )
    wide = jnp.where(same, wide, 0.0)
    kk[0] = wide.astype(BF16)
    kk[1] = (wide - wide.astype(BF16).astype(F32)).astype(BF16)
    for i in range(COUNT // NS):
        pot[i * NS : (i + 1) * NS] = jnp.broadcast_to(columns[:, i : i + 1], (NS, NS))
    for i in range(2):
        cell = lax.broadcasted_iota(jnp.int32, (NS, NS), 0) + i * NS
        value = jnp.broadcast_to(columns[:, 16 + i : 17 + i], (NS, NS))
        scale[i * NS : (i + 1) * NS] = jnp.where(8 * cell + 8 <= live, value, 0.0)
    span = (top_ref[0] - cut_ref[0]) * 0.5
    centre = (top_ref[0] + cut_ref[0]) * 0.5

    def gather_owned():
        for b in range(BLOCKS):
            at = min(b, 6) * FACE
            gath[b] = dot(g_own[b], ext[at : at + WIN]).astype(BF16)

    def gather_side(side):
        at = slice(side * FACE, (side + 1) * FACE)
        for b in range(BLOCKS):
            gath[b] = gath[b] + dot(g_gho[b, :, at], extg[at]).astype(BF16)

    def scatter_side(side):
        return halves(dot(t_gho[side * FACE : (side + 1) * FACE], loc[...]))

    def far_far():
        values = extg[FACE:]
        return halves(dot(a_far[0], values)) + dot(a_far[1], values[:, :NS])

    def apply_cells():
        for b in range(BLOCKS):
            for i in range(0, GROUPS, 2):
                one = gath[b, i * GROWS : (i + 1) * GROWS]
                two = gath[b, (i + 1) * GROWS : (i + 2) * GROWS]
                low = dot(kk[1], jnp.concatenate([one[:, :NS], two[:, :NS]], axis=1))
                for j, part in enumerate((one, two)):
                    r = b * GROUPS + i + j
                    out = halves(dot(kk[0], part)) + low[:, j * NS : (j + 1) * NS]
                    out = (out.reshape(SLOTS, 8, NS) * scale[r * 8 : r * 8 + 8][None]).reshape(GROWS, NS)
                    loc[r * GROWS : (r + 1) * GROWS] = split(out)

    def build_far():
        def far_block(h, carry):
            for t in range(2):
                b = 2 * h + t
                for i in range(GROUPS):
                    part = g_gho[b, i * GROWS : (i + 1) * GROWS, FACE:]
                    out = dot(kk[0], part) + dot(kk[1], part)
                    by = scale[pl.ds(pl.multiple_of(b * 8 * GROUPS + 8 * i, 8), 8)]
                    by = jnp.concatenate([by, by], axis=1)
                    out = (out.reshape(SLOTS, 8, FACE) * by[None]).reshape(GROWS, FACE)
                    out_hi = out.astype(BF16)
                    gath[b, i * GROWS : (i + 1) * GROWS] = out_hi
                    loc[pl.ds(pl.multiple_of(b * ROWS + i * GROWS, 16), GROWS)] = (
                        out - out_hi.astype(F32)
                    ).astype(BF16)
            return carry

        lax.fori_loop(0, BLOCKS // 2, far_block, 0)
        out = dot(t_gho[FACE:], gath[...].reshape(BLOCKS * ROWS, FACE)) + dot(t_gho[FACE:], loc[...])
        a_far[0] = out.astype(BF16)
        a_far[1] = (out - out.astype(BF16).astype(F32)).astype(BF16)

    def step(k, carry):
        alpha = jnp.where(k == 0, 1.0, 2.0) / span
        beta = jnp.where(k == 0, 0.0, 1.0)
        @pl.when(k == DEG)
        def _():
            corr_sum.start_first(quarters(dot(ext[...], ext[...], ((0,), (0,)))) * share)

        gather_owned()
        take_face(0)
        gather_side(0)

        @pl.when(k == 0)
        def _():
            take_face(1)
            gather_side(1)

        apply_cells()
        far_part[...] = scatter_side(1)

        @pl.when(k < DEG)
        def _():
            @pl.when(k == 0)
            def _():
                send_back(1, far_part[...])

            @pl.when(k > 0)
            def _():
                take_face(1)
                send_back(1, far_part[...] + far_far())
                gather_side(1)
                apply_cells()

            send_back(0, scatter_side(0))
            for j, (first, last) in enumerate(CHUNK_BLOCKS):
                at = slice(j * FACE, (j + 1) * FACE)
                lanes = slice(CHUNK_AT[j] * ROWS, (CHUNK_AT[j] + last - first) * ROWS)
                added = halves(dot(t_own[:, lanes], loc[first * ROWS : last * ROWS]))
                now = cur[at]
                new = alpha * (added + (pot[at] - centre) * now) - beta * prev[at]
                prev[at] = now
                cur[at] = new
                ext[at] = split(new)
            face_part[...] = halves(dot(pick[...], ext[...]))

            @pl.when(k == 0)
            def _():
                build_far()

            take_back(0, alpha)
            take_back(1, alpha)
            send_faces(face_part[...] + halves(dot(cross[...], extr[...])))
            for j in range(COUNT // FACE):
                at = slice(j * FACE, (j + 1) * FACE)
                new = cur[at] + halves(dot(pick_t[at], extr[...]))
                cur[at] = new
                ext[at] = split(new)

        return carry

    share = 1.0 / (total * COUNT)
    lax.fori_loop(0, DEG + 1, step, 0)

    corr_sum.start_second()
    gram_acc[...] = jnp.zeros((2 * NS, 2 * NS), F32)

    def gram_blocks(h, carry):
        part = gram_acc[...]
        for t in range(BLOCKS // 2):
            b = h * (BLOCKS // 2) + t
            rows = loc[pl.ds(pl.multiple_of(b * ROWS, NS), ROWS)]
            at = pl.ds(pl.multiple_of(b * FACE, FACE), FACE)
            part = part + dot(gath[b], rows, ((0,), (0,)))
            part = part + dot(ext[at], split(pot[at] * cur[at]), ((0,), (0,)))
        gram_acc[...] = part
        return carry

    lax.fori_loop(0, 2, gram_blocks, 0)
    take_face(1)
    mixed = quarters(dot(extg[FACE:], split(far_part[...] + 0.5 * far_far()), ((0,), (0,))))
    gram_sum.start_first((quarters(gram_acc[...]) + (mixed + mixed.T)) * share)
    corr_sum.start_third()
    gram_sum.start_second()
    left[...] = corr_sum.finish()
    right[...] = jnp.where(
        lax.broadcasted_iota(jnp.int32, (NS, NS), 0) == lax.broadcasted_iota(jnp.int32, (NS, NS), 1),
        1.0,
        0.0,
    ).astype(F32)
    def panel(p, carry):
        factor_panel(p, left, right, inverse)
        return carry

    lax.fori_loop(0, NS // 16, panel, 0)
    gram_sum.start_third()
    lax.fori_loop(NS // 16, NS // 8, panel, 0)
    inv = inverse[...]
    hi = inv.astype(BF16)
    low = (inv - hi.astype(F32)).astype(BF16)
    wide = jnp.concatenate([hi, hi], axis=1)
    narrow = jnp.concatenate([low, jnp.zeros_like(low)], axis=1)
    weights = jnp.concatenate([wide, narrow], axis=0)
    for j in range(COUNT // FACE):
        at = slice(j * FACE, (j + 1) * FACE)
        ortho_ref[at] = halves(dot(ext[at], weights, ((1,), (1,))))
    hgram = gram_sum.finish()
    rows_grid = n_grp // 4
    high = lax.Precision.HIGHEST
    r = grp // 4
    q = lax.rem(grp, 4)
    jump = 8 * rows_grid
    mine = jnp.concatenate(
        [inverse[pl.ds(pl.multiple_of(jump * t + 8 * r, 8), 8)] for t in range(NS // jump)], axis=0
    )
    other = jnp.concatenate(
        [inverse[pl.ds(pl.multiple_of(32 * t + 8 * q, 8), 8)] for t in range(NS // 32)], axis=0
    )
    mine = jnp.dot(mine, hgram, precision=high, preferred_element_type=F32)
    tile_ref[...] = lax.dot_general(
        mine, other, (((1,), (1,)), ((), ())), precision=high, preferred_element_type=F32
    )


def whole(n_dom, n_grp, operands):
    n_in, n_out = n_grp // 2, 2 * n_dom
    piece = NS // n_in
    rows_grid = n_grp // 4
    vmem = pl.BlockSpec(memory_space=pltpu.VMEM)
    smem = pl.BlockSpec(memory_space=pltpu.SMEM)
    dma = pltpu.SemaphoreType.DMA
    one_sum = [
        pltpu.VMEM((n_in, piece, NS), F32),
        pltpu.VMEM((n_in, piece, NS), F32),
        pltpu.VMEM((2, piece, NS), F32),
        pltpu.VMEM((n_out, piece, NS), F32),
        pltpu.VMEM((n_in, piece, NS), F32),
        dma((2, n_in)),
        dma((2, n_out)),
        dma((2, n_in)),
    ]
    faces = pltpu.VMEM((2, FACE, NS), F32)
    field = pltpu.VMEM((COUNT, NS), F32)
    return pl.pallas_call(
        functools.partial(filter_kernel, n_dom, n_grp),
        out_shape=(
            jax.ShapeDtypeStruct((COUNT, NS), F32),
            jax.ShapeDtypeStruct((NS // rows_grid, NS // 4), F32),
        ),
        in_specs=[smem] * 3 + [pl.BlockSpec(memory_space=pl.ANY)] + [vmem] * 5,
        out_specs=(vmem, vmem),
        scratch_shapes=[
            pltpu.VMEM((BLOCKS, ROWS, WIN), BF16),
            pltpu.VMEM((BLOCKS, ROWS, GHOST), BF16),
            pltpu.VMEM((FACE, CHUNK_ALL * ROWS), BF16),
            pltpu.VMEM((GHOST, BLOCKS * ROWS), BF16),
            pltpu.VMEM((2 * FACE, COUNT), BF16),
            pltpu.VMEM((COUNT, 2 * FACE), BF16),
            pltpu.VMEM((2 * FACE, 2 * FACE), BF16),
            pltpu.VMEM((2, GROWS, GROWS), BF16),
            pltpu.VMEM((BLOCKS, ROWS, 2 * NS), BF16),
            pltpu.VMEM((BLOCKS * ROWS, 2 * NS), BF16),
            pltpu.VMEM((COUNT, 2 * NS), BF16),
            pltpu.VMEM((GHOST, 2 * NS), BF16),
            pltpu.VMEM((GHOST, 2 * NS), BF16),
            pltpu.VMEM((2, FACE, FACE), BF16),
            field,
            field,
            field,
            pltpu.VMEM((2 * NS, NS), F32),
            pltpu.VMEM((2 * FACE, NS), F32),
            faces,
            faces,
            faces,
            faces,
            pltpu.VMEM((NS, NS), F32),
            pltpu.VMEM((NS, NS), F32),
            pltpu.VMEM((NS, NS), F32),
            pltpu.VMEM((BLOCKS, ROWS, NS), jnp.int32),
            pltpu.VMEM((BLOCKS, ROWS), jnp.int32),
            pltpu.VMEM((FACE, NS), F32),
            pltpu.VMEM((2 * NS, 2 * NS), F32),
            dma((2, 2)),
            dma((2, 2)),
            dma,
            *one_sum,
            *one_sum,
        ],
        compiler_params=pltpu.CompilerParams(
            collective_id=0, has_side_effects=True, vmem_limit_bytes=62 * 1024 * 1024
        ),
    )(*operands)


def body(
    states,
    potential,
    cell_scale,
    stiffness,
    connect,
    face_nodes,
    node_count,
    filter_cut,
    spectrum_top,
):
    return whole(
        lax.axis_size("dom"),
        lax.axis_size("grp"),
        (
            filter_cut,
            spectrum_top,
            node_count,
            states,
            potential.reshape(COUNT // NS, NS),
            cell_scale.reshape(CELLS // NS, NS),
            stiffness,
            connect,
            face_nodes,
        ),
    )


def solution(mesh):
    placed = (
        P(("dom", "grp"), None),
        P(("dom", "grp")),
        P(("dom", "grp")),
        P(),
        P(None, ("dom", "grp")),
        P(None, ("dom", "grp")),
        P(("dom", "grp")),
        P(),
        P(),
    )
    return jax.shard_map(
        body,
        mesh=mesh,
        in_specs=placed,
        out_specs=(P(("dom", "grp"), None), P("grp", None)),
        check_vma=False,
    )
```

```python
import functools

import jax
import jax.numpy as jnp
from jax import lax
from jax.experimental import pallas as pl
from jax.experimental.pallas import tpu as pltpu
from jax.sharding import PartitionSpec as P

NB = 8
NS = 128
NPC = 27
CELLS = 256
SLOTS = 28
DEG = 4
COUNT = 2048
FACE = 256
BLOCKS = 8
GROUPS = 4
GROWS = SLOTS * 8
ROWS = GROUPS * GROWS
WIN = 2 * FACE
GHOST = 2 * FACE

F32 = jnp.float32
BF16 = jnp.bfloat16
MESH = pl.DeviceIdType.MESH


def dot(a, b, dims=((1,), (0,))):
    return lax.dot_general(a, b, (dims, ((), ())), preferred_element_type=F32)


def split(x):
    hi = x.astype(BF16)
    lo = (x - hi.astype(F32)).astype(BF16)
    return jnp.concatenate([hi, lo], axis=1)


def halves(x):
    return x[:, :NS] + x[:, NS:]


def quarters(x):
    return (x[:NS, :NS] + x[NS:, NS:]) + (x[:NS, NS:] + x[NS:, :NS])


CHUNK_BLOCKS = ((0, 1), (0, 2), (1, 3), (2, 4), (3, 5), (4, 6), (5, 8), (6, 8))
CHUNK_AT = (0, 1, 3, 5, 7, 9, 11, 14)
CHUNK_ALL = 16


class Sum:
    def __init__(self, n_dom, n_grp, dom, grp, refs):
        self.src, self.slots, self.part, self.sums, self.out, self.sems1, self.sems2, self.sems3 = refs
        self.n_in = n_grp // 2
        self.n_out = 2 * n_dom
        self.inner = lax.rem(grp, self.n_in)
        self.outer = dom * 2 + grp // self.n_in

    def device(self, outer, inner):
        return (outer // 2, lax.rem(outer, 2) * self.n_in + inner)

    def in_partner(self, s):
        return lax.rem(self.inner + s, self.n_in)

    def partners(self):
        found = [self.device(self.outer, self.in_partner(s)) for s in range(1, self.n_in)]
        return found + [
            self.device(lax.rem(self.outer + s, self.n_out), self.inner) for s in range(1, self.n_out)
        ]

    def in_copy(self, s, src, dst, sems):
        return pltpu.make_async_remote_copy(
            src_ref=src, dst_ref=dst, send_sem=sems.at[0, s], recv_sem=sems.at[1, s],
            device_id=self.device(self.outer, self.in_partner(s)), device_id_type=MESH,
        )

    def first(self):
        return [
            self.in_copy(s, self.src.at[self.in_partner(s)], self.slots.at[s], self.sems1)
            for s in range(1, self.n_in)
        ]

    def second(self):
        return [
            pltpu.make_async_remote_copy(
                src_ref=self.part.at[0], dst_ref=self.sums.at[self.outer],
                send_sem=self.sems2.at[0, s], recv_sem=self.sems2.at[1, s],
                device_id=self.device(lax.rem(self.outer + s, self.n_out), self.inner),
                device_id_type=MESH,
            )
            for s in range(1, self.n_out)
        ]

    def third(self):
        return [
            self.in_copy(s, self.part.at[1], self.out.at[self.inner], self.sems3)
            for s in range(1, self.n_in)
        ]

    def start_first(self, value):
        piece = NS // self.n_in
        for j in range(self.n_in):
            self.src[j] = value[j * piece : (j + 1) * piece]
        for copy in self.first():
            copy.start()
        self.slots[0] = self.src[self.inner]

    def start_second(self):
        for copy in self.first():
            copy.wait()
        self.part[0] = jnp.sum(self.slots[...], axis=0)
        for copy in self.second():
            copy.start()
        self.sums[self.outer] = self.part[0]

    def start_third(self):
        for copy in self.second():
            copy.wait()
        self.part[1] = jnp.sum(self.sums[...], axis=0)
        for copy in self.third():
            copy.start()
        self.out[self.inner] = self.part[1]

    def finish(self):
        for copy in self.third():
            copy.wait()
        return self.out[...].reshape(NS, NS)


def dot_split(a, b, dim):
    a_hi = a.astype(BF16)
    a_lo = (a - a_hi.astype(F32)).astype(BF16)
    b_hi = b.astype(BF16)
    b_lo = (b - b_hi.astype(F32)).astype(BF16)
    return dot(
        jnp.concatenate([a_hi, a_lo, a_hi], axis=1),
        jnp.concatenate([b_hi, b_hi, b_lo], axis=dim),
        ((1,), (dim,)),
    )


def triple(x):
    hi = x.astype(BF16).astype(F32)
    rest = x - hi
    mid = rest.astype(BF16).astype(F32)
    return hi, mid, rest - mid


def factor_panel(p, left_ref, right_ref, inv_ref):
    sub = lax.broadcasted_iota(jnp.int32, (8, NS), 0)
    a = left_ref[:8]
    m = right_ref[:8]
    cols = [jnp.broadcast_to(a[:, k : k + 1], (8, NS)) for k in range(8)]
    pivots = jnp.ones((8, NS), F32)
    for j in range(8):
        at = [None] * j + [jnp.broadcast_to(cols[k][j : j + 1], (8, NS)) for k in range(j, 8)]
        mult = jnp.where(sub > j, cols[j] * (1.0 / at[j]), 0.0)
        for k in range(j + 1, 8):
            cols[k] = cols[k] - mult * at[k]
        a, m = (
            a - mult * jnp.broadcast_to(a[j : j + 1], (8, NS)),
            m - mult * jnp.broadcast_to(m[j : j + 1], (8, NS)),
        )
        pivots = jnp.where(sub == j, at[j], pivots)
    scale = 1.0 / jnp.sqrt(pivots)
    a, m = a * scale, m * scale
    inv_ref[pl.ds(pl.multiple_of(8 * p, 8), 8)] = m
    a = jnp.concatenate([a[:, 8:], jnp.zeros((8, 8), F32)], axis=1)
    hi, mid, low = triple(a)
    mhi, mmid, mlow = triple(m)
    one = jnp.concatenate([hi, hi, mid, hi, low, mid], axis=0).astype(BF16)
    two = jnp.concatenate([hi, mid, hi, low, hi, mid], axis=0)
    two_m = jnp.concatenate([mhi, mmid, mhi, mlow, mhi, mmid], axis=0)
    two = jnp.concatenate([two, two_m], axis=1).astype(BF16)
    both = dot(one, two, ((0,), (0,)))[: NS - 8]
    rest = left_ref[8:]
    rest = jnp.concatenate([rest[:, 8:], jnp.zeros((NS - 8, 8), F32)], axis=1)
    left_ref[: NS - 8] = rest - both[:, :NS]
    right_ref[: NS - 8] = right_ref[8:] - both[:, NS:]


def filter_kernel(
    n_dom,
    n_grp,
    cut_ref,
    top_ref,
    live_ref,
    states_ref,
    pot_ref,
    scale_ref,
    kmat_ref,
    conn_ref,
    face_ref,
    ortho_ref,
    tile_ref,
    g_own,
    g_gho,
    t_own,
    t_gho,
    pick,
    pick_t,
    cross,
    kk,
    gath,
    loc,
    ext,
    extg,
    extr,
    a_far,
    cur,
    prev,
    pot,
    scale,
    face_part,
    face_send,
    face_recv,
    back_send,
    back_recv,
    left,
    right,
    inverse,
    conn_col,
    conn_row,
    far_part,
    gram_acc,
    face_sems,
    back_sems,
    states_sem,
    *sums,
):
    dom = lax.axis_index("dom")
    grp = lax.axis_index("grp")
    total = n_dom * n_grp
    me = dom * n_grp + grp
    up = lax.rem(me + 1, total)
    down = lax.rem(me + total - 1, total)
    even = lax.rem(grp, 2) == 0
    near_at = jnp.where(even, up, down)
    far_at = jnp.where(even, down, up)
    ids = [(at // n_grp, lax.rem(at, n_grp)) for at in (near_at, far_at)]
    edge = jnp.logical_or(me == 0, me == total - 1)
    partners = list(ids)
    corr_sum = Sum(n_dom, n_grp, dom, grp, sums[: len(sums) // 2])
    gram_sum = Sum(n_dom, n_grp, dom, grp, sums[len(sums) // 2 :])
    partners += corr_sum.partners()
    states_copy = pltpu.make_async_copy(states_ref, cur, states_sem)
    states_copy.start()
    barrier = pltpu.get_barrier_semaphore()
    for device in partners:
        pl.semaphore_signal(barrier, inc=1, device_id=device, device_id_type=MESH)

    def swap(side, send, recv, sems):
        return pltpu.make_async_remote_copy(
            src_ref=send.at[side], dst_ref=recv.at[side],
            send_sem=sems.at[side, 0], recv_sem=sems.at[side, 1],
            device_id=ids[side], device_id_type=MESH,
        )

    def send_face(side, value):
        face_send[side] = value
        swap(side, face_send, face_recv, face_sems).start()

    def take_face(side):
        swap(side, face_send, face_recv, face_sems).wait()
        value = face_recv[side] if side == 0 else jnp.where(edge, 0.0, face_recv[side])
        extg[side * FACE : (side + 1) * FACE] = split(value)

    def send_back(side, value):
        back_send[side] = value
        swap(side, back_send, back_recv, back_sems).start()

    def take_back(side, alpha):
        swap(side, back_send, back_recv, back_sems).wait()
        value = back_recv[side] if side == 0 else jnp.where(edge, 0.0, back_recv[side])
        extr[side * FACE : (side + 1) * FACE] = split(alpha * value)

    live = live_ref[0]
    lower, upper = face_ref[0:1], face_ref[1:2]
    faces = [jnp.where(even, upper, lower), jnp.where(even, lower, upper)]
    face_rows = jnp.concatenate(
        [faces[0][:, :NS], faces[0][:, NS:], faces[1][:, :NS], faces[1][:, NS:]], axis=0
    ).astype(F32)
    stacked = jnp.concatenate(
        [pot_ref[...], scale_ref[...], face_rows, jnp.zeros((2, NS), F32)], axis=0
    )
    columns = stacked.T
    wants = jnp.concatenate([columns[:, c : c + 1] for c in (18, 19, 20, 21)], axis=0).astype(jnp.int32)
    wants = jnp.broadcast_to(wants, (2 * FACE, NS))

    def first_field(i, carry):
        start = pl.multiple_of(i * NS, NS)
        at = pl.ds(start, NS)
        node = lax.broadcasted_iota(jnp.int32, (NS, NS), 0) + start
        value = jnp.where(node < live, cur[at], 0.0)
        cur[at] = value
        prev[at] = jnp.zeros((NS, NS), F32)
        ext[at] = split(value)
        lane = lax.broadcasted_iota(jnp.int32, (2 * FACE, NS), 1) + start
        pick[:, at] = jnp.where(wants == lane, 1.0, 0.0).astype(BF16)
        return carry

    states_copy.wait()
    lax.fori_loop(0, COUNT // NS, first_field, 0)
    face_part[...] = halves(dot(pick[...], ext[...]))

    raw = jnp.concatenate([conn_ref[...], jnp.full((32 - NPC, CELLS), -1, jnp.int32)], axis=0)
    cell = lax.broadcasted_iota(jnp.int32, (32, CELLS), 1)
    start = jnp.minimum(cell // 32, 6) * FACE
    low_at = WIN + jnp.where(even, FACE, 0)
    high_at = WIN + jnp.where(even, 0, FACE)
    column = jnp.where(
        raw < FACE,
        raw + low_at,
        jnp.where(raw >= FACE + COUNT, raw - (FACE + COUNT) + high_at, raw - FACE - start),
    )
    column = jnp.where(raw < 0, -1, column)
    by_cell = column.astype(F32).T
    lane = lax.broadcasted_iota(jnp.int32, (ROWS, NS), 1)
    packed = jnp.zeros((ROWS, NS), F32)
    for b in range(BLOCKS):
        pieces = []
        for r in range(b * GROUPS, (b + 1) * GROUPS):
            pieces += [by_cell[8 * r : 8 * r + 8, a : a + 1] for a in range(SLOTS)]
        col = jnp.concatenate([jnp.broadcast_to(piece, (8, NS)) for piece in pieces], axis=0)
        conn_col[b] = col.astype(jnp.int32)
        packed = jnp.where(lane == b, col, packed)
    conn_row[...] = packed.T[:BLOCKS].astype(jnp.int32)

    pl.semaphore_wait(barrier, len(partners))
    send_face(1, face_part[FACE:])
    send_face(0, face_part[:FACE])

    def build(b, carry):
        col = conn_col[b]
        col = jnp.concatenate([col] * (WIN // NS), axis=1)
        lane = lax.broadcasted_iota(jnp.int32, (ROWS, WIN), 1)
        g_own[b] = jnp.where(col == lane, 1.0, 0.0).astype(BF16)
        g_gho[b] = jnp.where(col == lane + WIN, 1.0, 0.0).astype(BF16)
        row = conn_row[pl.ds(b, 1)]
        sub = lax.broadcasted_iota(jnp.int32, (WIN, ROWS), 0)
        gho = jnp.where(row == sub + WIN, 1.0, 0.0).astype(BF16)
        t_gho[:, pl.ds(pl.multiple_of(b * ROWS, NS), ROWS)] = gho
        own = jnp.where(row == sub, 1.0, 0.0).astype(BF16)
        at = jnp.where(b < 7, 2 * b, 13)
        t_own[:, pl.ds(pl.multiple_of(at * ROWS, NS), ROWS)] = own[:FACE]
        at = jnp.where(b < 6, 2 * b + 1, b + 8)
        t_own[:, pl.ds(pl.multiple_of(at * ROWS, NS), ROWS)] = own[FACE:]
        return carry

    lax.fori_loop(0, BLOCKS, build, 0)

    def build_pick(i, carry):
        start = pl.multiple_of(i * NS, NS)
        sub = lax.broadcasted_iota(jnp.int32, (NS, FACE), 0) + start
        for side in range(2):
            value = jnp.where(faces[side] == sub, 1.0, 0.0).astype(BF16)
            pick_t[pl.ds(start, NS), side * FACE : (side + 1) * FACE] = value
        return carry

    lax.fori_loop(0, COUNT // NS, build_pick, 0)
    for side in range(2):
        row = jnp.broadcast_to(faces[side], (2 * FACE, FACE))
        want = jnp.concatenate([wants, wants], axis=1)
        cross[:, side * FACE : (side + 1) * FACE] = jnp.where(want == row, 1.0, 0.0).astype(BF16)
    spread = (
        lax.broadcasted_iota(jnp.int32, (GROWS, NPC), 0) // 8
        == lax.broadcasted_iota(jnp.int32, (GROWS, NPC), 1)
    )
    spread = jnp.where(spread, 1.0, 0.0).astype(F32)
    wide = lax.dot_general(
        spread, kmat_ref[...], (((1,), (0,)), ((), ())),
        precision=lax.Precision.HIGHEST, preferred_element_type=F32,
    )
    wide = lax.dot_general(
        wide, spread, (((1,), (1,)), ((), ())),
        precision=lax.Precision.HIGHEST, preferred_element_type=F32,
    )
    same = lax.rem(lax.broadcasted_iota(jnp.int32, (GROWS, GROWS), 0), 8) == lax.rem(
        lax.broadcasted_iota(jnp.int32, (GROWS, GROWS), 1), 8
    )
    wide = jnp.where(same, wide, 0.0)
    kk[0] = wide.astype(BF16)
    kk[1] = (wide - wide.astype(BF16).astype(F32)).astype(BF16)
    for i in range(COUNT // NS):
        pot[i * NS : (i + 1) * NS] = jnp.broadcast_to(columns[:, i : i + 1], (NS, NS))
    for i in range(2):
        cell = lax.broadcasted_iota(jnp.int32, (NS, NS), 0) + i * NS
        value = jnp.broadcast_to(columns[:, 16 + i : 17 + i], (NS, NS))
        scale[i * NS : (i + 1) * NS] = jnp.where(8 * cell + 8 <= live, value, 0.0)
    span = (top_ref[0] - cut_ref[0]) * 0.5
    centre = (top_ref[0] + cut_ref[0]) * 0.5

    def gather_owned():
        for b in range(BLOCKS):
            at = min(b, 6) * FACE
            gath[b] = dot(g_own[b], ext[at : at + WIN]).astype(BF16)

    def gather_side(side):
        at = slice(side * FACE, (side + 1) * FACE)
        for b in range(BLOCKS):
            gath[b] = gath[b] + dot(g_gho[b, :, at], extg[at]).astype(BF16)

    def scatter_side(side):
        return halves(dot(t_gho[side * FACE : (side + 1) * FACE], loc[...]))

    def far_far():
        values = extg[FACE:]
        return halves(dot(a_far[0], values)) + dot(a_far[1], values[:, :NS])

    def apply_cells():
        for b in range(BLOCKS):
            for i in range(0, GROUPS, 2):
                one = gath[b, i * GROWS : (i + 1) * GROWS]
                two = gath[b, (i + 1) * GROWS : (i + 2) * GROWS]
                low = dot(kk[1], jnp.concatenate([one[:, :NS], two[:, :NS]], axis=1))
                for j, part in enumerate((one, two)):
                    r = b * GROUPS + i + j
                    out = halves(dot(kk[0], part)) + low[:, j * NS : (j + 1) * NS]
                    out = (out.reshape(SLOTS, 8, NS) * scale[r * 8 : r * 8 + 8][None]).reshape(GROWS, NS)
                    loc[r * GROWS : (r + 1) * GROWS] = split(out)

    def build_far():
        def far_block(h, carry):
            for t in range(2):
                b = 2 * h + t
                for i in range(GROUPS):
                    part = g_gho[b, i * GROWS : (i + 1) * GROWS, FACE:]
                    out = dot(kk[0], part) + dot(kk[1], part)
                    by = scale[pl.ds(pl.multiple_of(b * 8 * GROUPS + 8 * i, 8), 8)]
                    by = jnp.concatenate([by, by], axis=1)
                    out = (out.reshape(SLOTS, 8, FACE) * by[None]).reshape(GROWS, FACE)
                    out_hi = out.astype(BF16)
                    gath[b, i * GROWS : (i + 1) * GROWS] = out_hi
                    loc[pl.ds(pl.multiple_of(b * ROWS + i * GROWS, 16), GROWS)] = (
                        out - out_hi.astype(F32)
                    ).astype(BF16)
            return carry

        lax.fori_loop(0, BLOCKS // 2, far_block, 0)
        out = dot(t_gho[FACE:], gath[...].reshape(BLOCKS * ROWS, FACE)) + dot(t_gho[FACE:], loc[...])
        a_far[0] = out.astype(BF16)
        a_far[1] = (out - out.astype(BF16).astype(F32)).astype(BF16)

    def step(k, carry):
        alpha = jnp.where(k == 0, 1.0, 2.0) / span
        beta = jnp.where(k == 0, 0.0, 1.0)
        @pl.when(k == DEG)
        def _():
            corr_sum.start_first(quarters(dot(ext[...], ext[...], ((0,), (0,)))) * share)

        gather_owned()
        take_face(0)
        gather_side(0)

        @pl.when(k == 0)
        def _():
            take_face(1)
            gather_side(1)

        apply_cells()

        @pl.when(k == DEG)
        def _():
            corr_sum.start_second()

        far_part[...] = scatter_side(1)

        @pl.when(k < DEG)
        def _():
            @pl.when(k == 0)
            def _():
                send_back(1, far_part[...])

            @pl.when(k > 0)
            def _():
                take_face(1)
                send_back(1, far_part[...] + far_far())
                gather_side(1)
                apply_cells()

            send_back(0, scatter_side(0))
            for j, (first, last) in enumerate(CHUNK_BLOCKS):
                at = slice(j * FACE, (j + 1) * FACE)
                lanes = slice(CHUNK_AT[j] * ROWS, (CHUNK_AT[j] + last - first) * ROWS)
                added = halves(dot(t_own[:, lanes], loc[first * ROWS : last * ROWS]))
                now = cur[at]
                new = alpha * (added + (pot[at] - centre) * now) - beta * prev[at]
                prev[at] = now
                cur[at] = new
                ext[at] = split(new)
            face_part[...] = halves(dot(pick[...], ext[...]))

            @pl.when(k == 0)
            def _():
                build_far()

            take_back(0, alpha)
            take_back(1, alpha)
            for side in (1, 0):
                at = slice(side * FACE, (side + 1) * FACE)
                send_face(side, face_part[at] + halves(dot(cross[at], extr[...])))
            for j in range(COUNT // FACE):
                at = slice(j * FACE, (j + 1) * FACE)
                new = cur[at] + halves(dot(pick_t[at], extr[...]))
                cur[at] = new
                ext[at] = split(new)

        return carry

    share = 1.0 / (total * COUNT)
    lax.fori_loop(0, DEG + 1, step, 0)

    gram_acc[...] = jnp.zeros((2 * NS, 2 * NS), F32)

    def gram_blocks(h, carry):
        part = gram_acc[...]
        for t in range(BLOCKS // 2):
            b = h * (BLOCKS // 2) + t
            rows = loc[pl.ds(pl.multiple_of(b * ROWS, NS), ROWS)]
            at = pl.ds(pl.multiple_of(b * FACE, FACE), FACE)
            part = part + dot(gath[b], rows, ((0,), (0,)))
            part = part + dot(ext[at], split(pot[at] * cur[at]), ((0,), (0,)))
        gram_acc[...] = part
        return carry

    lax.fori_loop(0, 2, gram_blocks, 0)
    take_face(1)
    mixed = quarters(dot(extg[FACE:], split(far_part[...] + 0.5 * far_far()), ((0,), (0,))))
    gram_sum.start_first((quarters(gram_acc[...]) + (mixed + mixed.T)) * share)
    corr_sum.start_third()
    gram_sum.start_second()
    left[...] = corr_sum.finish()
    right[...] = jnp.where(
        lax.broadcasted_iota(jnp.int32, (NS, NS), 0) == lax.broadcasted_iota(jnp.int32, (NS, NS), 1),
        1.0,
        0.0,
    ).astype(F32)
    def panel(p, carry):
        factor_panel(p, left, right, inverse)
        return carry

    lax.fori_loop(0, 10, panel, 0)
    gram_sum.start_third()
    lax.fori_loop(10, NS // 8, panel, 0)
    inv = inverse[...]
    hi = inv.astype(BF16)
    low = (inv - hi.astype(F32)).astype(BF16)
    wide = jnp.concatenate([hi, hi], axis=1)
    narrow = jnp.concatenate([low, jnp.zeros_like(low)], axis=1)
    weights = jnp.concatenate([wide, narrow], axis=0)
    for j in range(COUNT // FACE):
        at = slice(j * FACE, (j + 1) * FACE)
        ortho_ref[at] = halves(dot(ext[at], weights, ((1,), (1,))))
    hgram = gram_sum.finish()
    rows_grid = n_grp // 4
    r = grp // 4
    q = lax.rem(grp, 4)
    jump = 8 * rows_grid
    mine = jnp.concatenate(
        [inverse[pl.ds(pl.multiple_of(jump * t + 8 * r, 8), 8)] for t in range(NS // jump)], axis=0
    )
    other = jnp.concatenate(
        [inverse[pl.ds(pl.multiple_of(32 * t + 8 * q, 8), 8)] for t in range(NS // 32)], axis=0
    )
    mine = dot_split(mine, hgram, 0)
    tile_ref[...] = dot_split(mine, other, 1)


def whole(n_dom, n_grp, operands):
    n_in, n_out = n_grp // 2, 2 * n_dom
    piece = NS // n_in
    rows_grid = n_grp // 4
    vmem = pl.BlockSpec(memory_space=pltpu.VMEM)
    smem = pl.BlockSpec(memory_space=pltpu.SMEM)
    dma = pltpu.SemaphoreType.DMA
    one_sum = [
        pltpu.VMEM((n_in, piece, NS), F32),
        pltpu.VMEM((n_in, piece, NS), F32),
        pltpu.VMEM((2, piece, NS), F32),
        pltpu.VMEM((n_out, piece, NS), F32),
        pltpu.VMEM((n_in, piece, NS), F32),
        dma((2, n_in)),
        dma((2, n_out)),
        dma((2, n_in)),
    ]
    faces = pltpu.VMEM((2, FACE, NS), F32)
    field = pltpu.VMEM((COUNT, NS), F32)
    return pl.pallas_call(
        functools.partial(filter_kernel, n_dom, n_grp),
        out_shape=(
            jax.ShapeDtypeStruct((COUNT, NS), F32),
            jax.ShapeDtypeStruct((NS // rows_grid, NS // 4), F32),
        ),
        in_specs=[smem] * 3 + [pl.BlockSpec(memory_space=pl.ANY)] + [vmem] * 5,
        out_specs=(vmem, vmem),
        scratch_shapes=[
            pltpu.VMEM((BLOCKS, ROWS, WIN), BF16),
            pltpu.VMEM((BLOCKS, ROWS, GHOST), BF16),
            pltpu.VMEM((FACE, CHUNK_ALL * ROWS), BF16),
            pltpu.VMEM((GHOST, BLOCKS * ROWS), BF16),
            pltpu.VMEM((2 * FACE, COUNT), BF16),
            pltpu.VMEM((COUNT, 2 * FACE), BF16),
            pltpu.VMEM((2 * FACE, 2 * FACE), BF16),
            pltpu.VMEM((2, GROWS, GROWS), BF16),
            pltpu.VMEM((BLOCKS, ROWS, 2 * NS), BF16),
            pltpu.VMEM((BLOCKS * ROWS, 2 * NS), BF16),
            pltpu.VMEM((COUNT, 2 * NS), BF16),
            pltpu.VMEM((GHOST, 2 * NS), BF16),
            pltpu.VMEM((GHOST, 2 * NS), BF16),
            pltpu.VMEM((2, FACE, FACE), BF16),
            field,
            field,
            field,
            pltpu.VMEM((2 * NS, NS), F32),
            pltpu.VMEM((2 * FACE, NS), F32),
            faces,
            faces,
            faces,
            faces,
            pltpu.VMEM((NS, NS), F32),
            pltpu.VMEM((NS, NS), F32),
            pltpu.VMEM((NS, NS), F32),
            pltpu.VMEM((BLOCKS, ROWS, NS), jnp.int32),
            pltpu.VMEM((BLOCKS, ROWS), jnp.int32),
            pltpu.VMEM((FACE, NS), F32),
            pltpu.VMEM((2 * NS, 2 * NS), F32),
            dma((2, 2)),
            dma((2, 2)),
            dma,
            *one_sum,
            *one_sum,
        ],
        compiler_params=pltpu.CompilerParams(
            collective_id=0, has_side_effects=True, vmem_limit_bytes=62 * 1024 * 1024
        ),
    )(*operands)


def body(
    states,
    potential,
    cell_scale,
    stiffness,
    connect,
    face_nodes,
    node_count,
    filter_cut,
    spectrum_top,
):
    return whole(
        lax.axis_size("dom"),
        lax.axis_size("grp"),
        (
            filter_cut,
            spectrum_top,
            node_count,
            states,
            potential.reshape(COUNT // NS, NS),
            cell_scale.reshape(CELLS // NS, NS),
            stiffness,
            connect,
            face_nodes,
        ),
    )


def solution(mesh):
    placed = (
        P(("dom", "grp"), None),
        P(("dom", "grp")),
        P(("dom", "grp")),
        P(),
        P(None, ("dom", "grp")),
        P(None, ("dom", "grp")),
        P(("dom", "grp")),
        P(),
        P(),
    )
    return jax.shard_map(
        body,
        mesh=mesh,
        in_specs=placed,
        out_specs=(P(("dom", "grp"), None), P("grp", None)),
        check_vma=False,
    )
```

```python
import functools

import jax
import jax.numpy as jnp
from jax import lax
from jax.experimental import pallas as pl
from jax.experimental.pallas import tpu as pltpu
from jax.sharding import PartitionSpec as P

NB = 8
NS = 128
NPC = 27
CELLS = 256
SLOTS = 28
DEG = 4
COUNT = 2048
FACE = 256
BLOCKS = 8
GROUPS = 4
GROWS = SLOTS * 8
ROWS = GROUPS * GROWS
WIN = 2 * FACE
GHOST = 2 * FACE

F32 = jnp.float32
BF16 = jnp.bfloat16
MESH = pl.DeviceIdType.MESH


def dot(a, b, dims=((1,), (0,))):
    return lax.dot_general(a, b, (dims, ((), ())), preferred_element_type=F32)


def split(x):
    hi = x.astype(BF16)
    lo = (x - hi.astype(F32)).astype(BF16)
    return jnp.concatenate([hi, lo], axis=1)


def halves(x):
    return x[:, :NS] + x[:, NS:]


def quarters(x):
    return (x[:NS, :NS] + x[NS:, NS:]) + (x[:NS, NS:] + x[NS:, :NS])


CHUNK_BLOCKS = ((0, 1), (0, 2), (1, 3), (2, 4), (3, 5), (4, 6), (5, 8), (6, 8))
CHUNK_AT = (0, 1, 3, 5, 7, 9, 11, 14)
CHUNK_ALL = 16


class Sum:
    def __init__(self, n_dom, n_grp, dom, grp, refs):
        self.src, self.slots, self.part, self.sums, self.out, self.sems1, self.sems2, self.sems3 = refs
        self.n_in = n_grp // 2
        self.n_out = 2 * n_dom
        self.inner = lax.rem(grp, self.n_in)
        self.outer = dom * 2 + grp // self.n_in

    def device(self, outer, inner):
        return (outer // 2, lax.rem(outer, 2) * self.n_in + inner)

    def in_partner(self, s):
        return lax.rem(self.inner + s, self.n_in)

    def partners(self):
        found = [self.device(self.outer, self.in_partner(s)) for s in range(1, self.n_in)]
        return found + [
            self.device(lax.rem(self.outer + s, self.n_out), self.inner) for s in range(1, self.n_out)
        ]

    def in_copy(self, s, src, dst, sems):
        return pltpu.make_async_remote_copy(
            src_ref=src, dst_ref=dst, send_sem=sems.at[0, s], recv_sem=sems.at[1, s],
            device_id=self.device(self.outer, self.in_partner(s)), device_id_type=MESH,
        )

    def first(self):
        return [
            self.in_copy(s, self.src.at[self.in_partner(s)], self.slots.at[s], self.sems1)
            for s in range(1, self.n_in)
        ]

    def second(self):
        return [
            pltpu.make_async_remote_copy(
                src_ref=self.part.at[0], dst_ref=self.sums.at[self.outer],
                send_sem=self.sems2.at[0, s], recv_sem=self.sems2.at[1, s],
                device_id=self.device(lax.rem(self.outer + s, self.n_out), self.inner),
                device_id_type=MESH,
            )
            for s in range(1, self.n_out)
        ]

    def third(self):
        return [
            self.in_copy(s, self.part.at[1], self.out.at[self.inner], self.sems3)
            for s in range(1, self.n_in)
        ]

    def start_first(self, value):
        piece = NS // self.n_in
        for j in range(self.n_in):
            self.src[j] = value[j * piece : (j + 1) * piece]
        for copy in self.first():
            copy.start()
        self.slots[0] = self.src[self.inner]

    def start_second(self):
        for copy in self.first():
            copy.wait()
        self.part[0] = jnp.sum(self.slots[...], axis=0)
        for copy in self.second():
            copy.start()
        self.sums[self.outer] = self.part[0]

    def start_third(self):
        for copy in self.second():
            copy.wait()
        self.part[1] = jnp.sum(self.sums[...], axis=0)
        for copy in self.third():
            copy.start()
        self.out[self.inner] = self.part[1]

    def finish(self):
        for copy in self.third():
            copy.wait()
        return self.out[...].reshape(NS, NS)


def dot_split(a, b, dim):
    a_hi = a.astype(BF16)
    a_lo = (a - a_hi.astype(F32)).astype(BF16)
    b_hi = b.astype(BF16)
    b_lo = (b - b_hi.astype(F32)).astype(BF16)
    return dot(
        jnp.concatenate([a_hi, a_lo, a_hi], axis=1),
        jnp.concatenate([b_hi, b_hi, b_lo], axis=dim),
        ((1,), (dim,)),
    )


def triple(x):
    hi = x.astype(BF16).astype(F32)
    rest = x - hi
    mid = rest.astype(BF16).astype(F32)
    return hi, mid, rest - mid


def factor_panel(p, left_ref, right_ref, inv_ref):
    sub = lax.broadcasted_iota(jnp.int32, (8, NS), 0)
    a = left_ref[:8]
    m = right_ref[:8]
    cols = [jnp.broadcast_to(a[:, k : k + 1], (8, NS)) for k in range(8)]
    pivots = jnp.ones((8, NS), F32)
    for j in range(8):
        at = [None] * j + [jnp.broadcast_to(cols[k][j : j + 1], (8, NS)) for k in range(j, 8)]
        mult = jnp.where(sub > j, cols[j] * (1.0 / at[j]), 0.0)
        for k in range(j + 1, 8):
            cols[k] = cols[k] - mult * at[k]
        a, m = (
            a - mult * jnp.broadcast_to(a[j : j + 1], (8, NS)),
            m - mult * jnp.broadcast_to(m[j : j + 1], (8, NS)),
        )
        pivots = jnp.where(sub == j, at[j], pivots)
    scale = 1.0 / jnp.sqrt(pivots)
    a, m = a * scale, m * scale
    inv_ref[pl.ds(pl.multiple_of(8 * p, 8), 8)] = m
    a = jnp.concatenate([a[:, 8:], jnp.zeros((8, 8), F32)], axis=1)
    hi, mid, low = triple(a)
    mhi, mmid, mlow = triple(m)
    one = jnp.concatenate([hi, hi, mid, hi, low, mid], axis=0).astype(BF16)
    two = jnp.concatenate([hi, mid, hi, low, hi, mid], axis=0)
    two_m = jnp.concatenate([mhi, mmid, mhi, mlow, mhi, mmid], axis=0)
    two = jnp.concatenate([two, two_m], axis=1).astype(BF16)
    both = dot(one, two, ((0,), (0,)))[: NS - 8]
    rest = left_ref[8:]
    rest = jnp.concatenate([rest[:, 8:], jnp.zeros((NS - 8, 8), F32)], axis=1)
    left_ref[: NS - 8] = rest - both[:, :NS]
    right_ref[: NS - 8] = right_ref[8:] - both[:, NS:]


def filter_kernel(
    n_dom,
    n_grp,
    cut_ref,
    top_ref,
    live_ref,
    states_ref,
    pot_ref,
    scale_ref,
    kmat_ref,
    conn_ref,
    face_ref,
    ortho_ref,
    tile_ref,
    g_own,
    g_gho,
    t_own,
    t_gho,
    pick,
    pick_t,
    cross,
    kk,
    gath,
    loc,
    ext,
    extg,
    extr,
    a_far,
    cur,
    prev,
    pot,
    scale,
    face_part,
    face_send,
    face_recv,
    back_send,
    back_recv,
    left,
    right,
    inverse,
    conn_col,
    conn_row,
    far_part,
    gram_acc,
    face_sems,
    back_sems,
    states_sem,
    *sums,
):
    dom = lax.axis_index("dom")
    grp = lax.axis_index("grp")
    total = n_dom * n_grp
    me = dom * n_grp + grp
    up = lax.rem(me + 1, total)
    down = lax.rem(me + total - 1, total)
    even = lax.rem(grp, 2) == 0
    near_at = jnp.where(even, up, down)
    far_at = jnp.where(even, down, up)
    ids = [(at // n_grp, lax.rem(at, n_grp)) for at in (near_at, far_at)]
    edge = jnp.logical_or(me == 0, me == total - 1)
    partners = list(ids)
    corr_sum = Sum(n_dom, n_grp, dom, grp, sums[: len(sums) // 2])
    gram_sum = Sum(n_dom, n_grp, dom, grp, sums[len(sums) // 2 :])
    partners += corr_sum.partners()
    states_copy = pltpu.make_async_copy(states_ref, cur, states_sem)
    states_copy.start()
    barrier = pltpu.get_barrier_semaphore()
    for device in partners:
        pl.semaphore_signal(barrier, inc=1, device_id=device, device_id_type=MESH)

    def swap(side, send, recv, sems):
        return pltpu.make_async_remote_copy(
            src_ref=send.at[side], dst_ref=recv.at[side],
            send_sem=sems.at[side, 0], recv_sem=sems.at[side, 1],
            device_id=ids[side], device_id_type=MESH,
        )

    def send_face(side, value):
        face_send[side] = value
        swap(side, face_send, face_recv, face_sems).start()

    def take_face(side):
        swap(side, face_send, face_recv, face_sems).wait()
        value = face_recv[side] if side == 0 else jnp.where(edge, 0.0, face_recv[side])
        extg[side * FACE : (side + 1) * FACE] = split(value)

    def send_back(side, value):
        back_send[side] = value
        swap(side, back_send, back_recv, back_sems).start()

    def take_back(side, alpha):
        swap(side, back_send, back_recv, back_sems).wait()
        value = back_recv[side] if side == 0 else jnp.where(edge, 0.0, back_recv[side])
        extr[side * FACE : (side + 1) * FACE] = split(alpha * value)

    live = live_ref[0]
    lower, upper = face_ref[0:1], face_ref[1:2]
    faces = [jnp.where(even, upper, lower), jnp.where(even, lower, upper)]
    face_rows = jnp.concatenate(
        [faces[0][:, :NS], faces[0][:, NS:], faces[1][:, :NS], faces[1][:, NS:]], axis=0
    ).astype(F32)
    stacked = jnp.concatenate(
        [pot_ref[...], scale_ref[...], face_rows, jnp.zeros((2, NS), F32)], axis=0
    )
    columns = stacked.T
    wants = jnp.concatenate([columns[:, c : c + 1] for c in (18, 19, 20, 21)], axis=0).astype(jnp.int32)
    wants = jnp.broadcast_to(wants, (2 * FACE, NS))

    def first_field(i, carry):
        start = pl.multiple_of(i * NS, NS)
        at = pl.ds(start, NS)
        node = lax.broadcasted_iota(jnp.int32, (NS, NS), 0) + start
        value = jnp.where(node < live, cur[at], 0.0)
        cur[at] = value
        prev[at] = jnp.zeros((NS, NS), F32)
        ext[at] = split(value)
        lane = lax.broadcasted_iota(jnp.int32, (2 * FACE, NS), 1) + start
        pick[:, at] = jnp.where(wants == lane, 1.0, 0.0).astype(BF16)
        return carry

    states_copy.wait()
    lax.fori_loop(0, COUNT // NS, first_field, 0)
    face_part[...] = halves(dot(pick[...], ext[...]))

    raw = jnp.concatenate([conn_ref[...], jnp.full((32 - NPC, CELLS), -1, jnp.int32)], axis=0)
    cell = lax.broadcasted_iota(jnp.int32, (32, CELLS), 1)
    start = jnp.minimum(cell // 32, 6) * FACE
    low_at = WIN + jnp.where(even, FACE, 0)
    high_at = WIN + jnp.where(even, 0, FACE)
    column = jnp.where(
        raw < FACE,
        raw + low_at,
        jnp.where(raw >= FACE + COUNT, raw - (FACE + COUNT) + high_at, raw - FACE - start),
    )
    column = jnp.where(raw < 0, -1, column)
    by_cell = column.astype(F32).T
    lane = lax.broadcasted_iota(jnp.int32, (ROWS, NS), 1)
    packed = jnp.zeros((ROWS, NS), F32)
    for b in range(BLOCKS):
        pieces = []
        for r in range(b * GROUPS, (b + 1) * GROUPS):
            pieces += [by_cell[8 * r : 8 * r + 8, a : a + 1] for a in range(SLOTS)]
        col = jnp.concatenate([jnp.broadcast_to(piece, (8, NS)) for piece in pieces], axis=0)
        conn_col[b] = col.astype(jnp.int32)
        packed = jnp.where(lane == b, col, packed)
    conn_row[...] = packed.T[:BLOCKS].astype(jnp.int32)

    pl.semaphore_wait(barrier, len(partners))
    send_face(1, face_part[FACE:])
    send_face(0, face_part[:FACE])

    def build(b, carry):
        col = conn_col[b]
        col = jnp.concatenate([col] * (WIN // NS), axis=1)
        lane = lax.broadcasted_iota(jnp.int32, (ROWS, WIN), 1)
        g_own[b] = jnp.where(col == lane, 1.0, 0.0).astype(BF16)
        g_gho[b] = jnp.where(col == lane + WIN, 1.0, 0.0).astype(BF16)
        row = conn_row[pl.ds(b, 1)]
        sub = lax.broadcasted_iota(jnp.int32, (WIN, ROWS), 0)
        gho = jnp.where(row == sub + WIN, 1.0, 0.0).astype(BF16)
        t_gho[:, pl.ds(pl.multiple_of(b * ROWS, NS), ROWS)] = gho
        own = jnp.where(row == sub, 1.0, 0.0).astype(BF16)
        at = jnp.where(b < 7, 2 * b, 13)
        t_own[:, pl.ds(pl.multiple_of(at * ROWS, NS), ROWS)] = own[:FACE]
        at = jnp.where(b < 6, 2 * b + 1, b + 8)
        t_own[:, pl.ds(pl.multiple_of(at * ROWS, NS), ROWS)] = own[FACE:]
        return carry

    lax.fori_loop(0, BLOCKS, build, 0)

    def build_pick(i, carry):
        start = pl.multiple_of(i * NS, NS)
        sub = lax.broadcasted_iota(jnp.int32, (NS, FACE), 0) + start
        for side in range(2):
            value = jnp.where(faces[side] == sub, 1.0, 0.0).astype(BF16)
            pick_t[pl.ds(start, NS), side * FACE : (side + 1) * FACE] = value
        return carry

    lax.fori_loop(0, COUNT // NS, build_pick, 0)
    for side in range(2):
        row = jnp.broadcast_to(faces[side], (2 * FACE, FACE))
        want = jnp.concatenate([wants, wants], axis=1)
        cross[:, side * FACE : (side + 1) * FACE] = jnp.where(want == row, 1.0, 0.0).astype(BF16)
    spread = (
        lax.broadcasted_iota(jnp.int32, (GROWS, NPC), 0) // 8
        == lax.broadcasted_iota(jnp.int32, (GROWS, NPC), 1)
    )
    spread = jnp.where(spread, 1.0, 0.0).astype(F32)
    wide = lax.dot_general(
        spread, kmat_ref[...], (((1,), (0,)), ((), ())),
        precision=lax.Precision.HIGHEST, preferred_element_type=F32,
    )
    wide = lax.dot_general(
        wide, spread, (((1,), (1,)), ((), ())),
        precision=lax.Precision.HIGHEST, preferred_element_type=F32,
    )
    same = lax.rem(lax.broadcasted_iota(jnp.int32, (GROWS, GROWS), 0), 8) == lax.rem(
        lax.broadcasted_iota(jnp.int32, (GROWS, GROWS), 1), 8
    )
    wide = jnp.where(same, wide, 0.0)
    kk[0] = wide.astype(BF16)
    kk[1] = (wide - wide.astype(BF16).astype(F32)).astype(BF16)
    for i in range(COUNT // NS):
        pot[i * NS : (i + 1) * NS] = jnp.broadcast_to(columns[:, i : i + 1], (NS, NS))
    for i in range(2):
        cell = lax.broadcasted_iota(jnp.int32, (NS, NS), 0) + i * NS
        value = jnp.broadcast_to(columns[:, 16 + i : 17 + i], (NS, NS))
        scale[i * NS : (i + 1) * NS] = jnp.where(8 * cell + 8 <= live, value, 0.0)
    span = (top_ref[0] - cut_ref[0]) * 0.5
    centre = (top_ref[0] + cut_ref[0]) * 0.5

    def gather_owned():
        for b in range(BLOCKS):
            at = min(b, 6) * FACE
            gath[b] = dot(g_own[b], ext[at : at + WIN]).astype(BF16)

    def gather_side(side):
        at = slice(side * FACE, (side + 1) * FACE)
        for b in range(BLOCKS):
            gath[b] = gath[b] + dot(g_gho[b, :, at], extg[at]).astype(BF16)

    def scatter_side(side):
        return halves(dot(t_gho[side * FACE : (side + 1) * FACE], loc[...]))

    def far_far():
        values = extg[FACE:]
        return halves(dot(a_far[0], values)) + dot(a_far[1], values[:, :NS])

    def apply_cells():
        for b in range(BLOCKS):
            for i in range(0, GROUPS, 2):
                one = gath[b, i * GROWS : (i + 1) * GROWS]
                two = gath[b, (i + 1) * GROWS : (i + 2) * GROWS]
                low = dot(kk[1], jnp.concatenate([one[:, :NS], two[:, :NS]], axis=1))
                for j, part in enumerate((one, two)):
                    r = b * GROUPS + i + j
                    out = halves(dot(kk[0], part)) + low[:, j * NS : (j + 1) * NS]
                    out = (out.reshape(SLOTS, 8, NS) * scale[r * 8 : r * 8 + 8][None]).reshape(GROWS, NS)
                    loc[r * GROWS : (r + 1) * GROWS] = split(out)

    def build_far():
        def far_block(h, carry):
            for t in range(BLOCKS // 2):
                b = h * (BLOCKS // 2) + t
                for i in range(GROUPS):
                    part = g_gho[b, i * GROWS : (i + 1) * GROWS, FACE:]
                    out = dot(kk[0], part) + dot(kk[1], part)
                    by = scale[pl.ds(pl.multiple_of(b * 8 * GROUPS + 8 * i, 8), 8)]
                    by = jnp.concatenate([by, by], axis=1)
                    out = (out.reshape(SLOTS, 8, FACE) * by[None]).reshape(GROWS, FACE)
                    out_hi = out.astype(BF16)
                    gath[b, i * GROWS : (i + 1) * GROWS] = out_hi
                    loc[pl.ds(pl.multiple_of(b * ROWS + i * GROWS, 16), GROWS)] = (
                        out - out_hi.astype(F32)
                    ).astype(BF16)
            return carry

        lax.fori_loop(0, 2, far_block, 0)
        out = dot(t_gho[FACE:], gath[...].reshape(BLOCKS * ROWS, FACE)) + dot(t_gho[FACE:], loc[...])
        a_far[0] = out.astype(BF16)
        a_far[1] = (out - out.astype(BF16).astype(F32)).astype(BF16)

    def step(k, carry):
        alpha = jnp.where(k == 0, 1.0, 2.0) / span
        beta = jnp.where(k == 0, 0.0, 1.0)
        @pl.when(k == DEG)
        def _():
            corr_sum.start_first(quarters(dot(ext[...], ext[...], ((0,), (0,)))) * share)

        gather_owned()
        take_face(0)
        gather_side(0)

        @pl.when(k == 0)
        def _():
            take_face(1)
            gather_side(1)

        apply_cells()

        @pl.when(k == DEG)
        def _():
            corr_sum.start_second()

        far_part[...] = scatter_side(1)

        @pl.when(k < DEG)
        def _():
            @pl.when(k == 0)
            def _():
                send_back(1, far_part[...])

            @pl.when(k > 0)
            def _():
                take_face(1)
                send_back(1, far_part[...] + far_far())
                gather_side(1)
                apply_cells()

            send_back(0, scatter_side(0))
            for j, (first, last) in enumerate(CHUNK_BLOCKS):
                at = slice(j * FACE, (j + 1) * FACE)
                lanes = slice(CHUNK_AT[j] * ROWS, (CHUNK_AT[j] + last - first) * ROWS)
                added = halves(dot(t_own[:, lanes], loc[first * ROWS : last * ROWS]))
                now = cur[at]
                new = alpha * (added + (pot[at] - centre) * now) - beta * prev[at]
                prev[at] = now
                cur[at] = new
                ext[at] = split(new)
            face_part[...] = halves(dot(pick[...], ext[...]))

            @pl.when(k == 0)
            def _():
                build_far()

            take_back(0, alpha)
            take_back(1, alpha)
            for side in (1, 0):
                at = slice(side * FACE, (side + 1) * FACE)
                send_face(side, face_part[at] + halves(dot(cross[at], extr[...])))
            for j in range(COUNT // FACE):
                at = slice(j * FACE, (j + 1) * FACE)
                new = cur[at] + halves(dot(pick_t[at], extr[...]))
                cur[at] = new
                ext[at] = split(new)

        return carry

    share = 1.0 / (total * COUNT)
    lax.fori_loop(0, DEG + 1, step, 0)

    gram_acc[...] = jnp.zeros((2 * NS, 2 * NS), F32)

    def gram_blocks(h, carry):
        part = gram_acc[...]
        for t in range(BLOCKS // 2):
            b = h * (BLOCKS // 2) + t
            rows = loc[pl.ds(pl.multiple_of(b * ROWS, NS), ROWS)]
            at = pl.ds(pl.multiple_of(b * FACE, FACE), FACE)
            part = part + dot(gath[b], rows, ((0,), (0,)))
            part = part + dot(ext[at], split(pot[at] * cur[at]), ((0,), (0,)))
        gram_acc[...] = part
        return carry

    lax.fori_loop(0, 2, gram_blocks, 0)
    take_face(1)
    mixed = quarters(dot(extg[FACE:], split(far_part[...] + 0.5 * far_far()), ((0,), (0,))))
    gram_sum.start_first((quarters(gram_acc[...]) + (mixed + mixed.T)) * share)
    corr_sum.start_third()
    gram_sum.start_second()
    left[...] = corr_sum.finish()
    right[...] = jnp.where(
        lax.broadcasted_iota(jnp.int32, (NS, NS), 0) == lax.broadcasted_iota(jnp.int32, (NS, NS), 1),
        1.0,
        0.0,
    ).astype(F32)
    def panel(p, carry):
        factor_panel(p, left, right, inverse)
        return carry

    lax.fori_loop(0, 10, panel, 0)
    gram_sum.start_third()
    lax.fori_loop(10, NS // 8, panel, 0)
    inv = inverse[...]
    hi = inv.astype(BF16)
    low = (inv - hi.astype(F32)).astype(BF16)
    wide = jnp.concatenate([hi, hi], axis=1)
    narrow = jnp.concatenate([low, jnp.zeros_like(low)], axis=1)
    weights = jnp.concatenate([wide, narrow], axis=0)
    for j in range(COUNT // FACE):
        at = slice(j * FACE, (j + 1) * FACE)
        ortho_ref[at] = halves(dot(ext[at], weights, ((1,), (1,))))
    hgram = gram_sum.finish()
    rows_grid = n_grp // 4
    r = grp // 4
    q = lax.rem(grp, 4)
    jump = 8 * rows_grid
    mine = jnp.concatenate(
        [inverse[pl.ds(pl.multiple_of(jump * t + 8 * r, 8), 8)] for t in range(NS // jump)], axis=0
    )
    other = jnp.concatenate(
        [inverse[pl.ds(pl.multiple_of(32 * t + 8 * q, 8), 8)] for t in range(NS // 32)], axis=0
    )
    mine = dot_split(mine, hgram, 0)
    tile_ref[...] = dot_split(mine, other, 1)


def whole(n_dom, n_grp, operands):
    n_in, n_out = n_grp // 2, 2 * n_dom
    piece = NS // n_in
    rows_grid = n_grp // 4
    vmem = pl.BlockSpec(memory_space=pltpu.VMEM)
    smem = pl.BlockSpec(memory_space=pltpu.SMEM)
    dma = pltpu.SemaphoreType.DMA
    one_sum = [
        pltpu.VMEM((n_in, piece, NS), F32),
        pltpu.VMEM((n_in, piece, NS), F32),
        pltpu.VMEM((2, piece, NS), F32),
        pltpu.VMEM((n_out, piece, NS), F32),
        pltpu.VMEM((n_in, piece, NS), F32),
        dma((2, n_in)),
        dma((2, n_out)),
        dma((2, n_in)),
    ]
    faces = pltpu.VMEM((2, FACE, NS), F32)
    field = pltpu.VMEM((COUNT, NS), F32)
    return pl.pallas_call(
        functools.partial(filter_kernel, n_dom, n_grp),
        out_shape=(
            jax.ShapeDtypeStruct((COUNT, NS), F32),
            jax.ShapeDtypeStruct((NS // rows_grid, NS // 4), F32),
        ),
        in_specs=[smem] * 3 + [pl.BlockSpec(memory_space=pl.ANY)] + [vmem] * 5,
        out_specs=(vmem, vmem),
        scratch_shapes=[
            pltpu.VMEM((BLOCKS, ROWS, WIN), BF16),
            pltpu.VMEM((BLOCKS, ROWS, GHOST), BF16),
            pltpu.VMEM((FACE, CHUNK_ALL * ROWS), BF16),
            pltpu.VMEM((GHOST, BLOCKS * ROWS), BF16),
            pltpu.VMEM((2 * FACE, COUNT), BF16),
            pltpu.VMEM((COUNT, 2 * FACE), BF16),
            pltpu.VMEM((2 * FACE, 2 * FACE), BF16),
            pltpu.VMEM((2, GROWS, GROWS), BF16),
            pltpu.VMEM((BLOCKS, ROWS, 2 * NS), BF16),
            pltpu.VMEM((BLOCKS * ROWS, 2 * NS), BF16),
            pltpu.VMEM((COUNT, 2 * NS), BF16),
            pltpu.VMEM((GHOST, 2 * NS), BF16),
            pltpu.VMEM((GHOST, 2 * NS), BF16),
            pltpu.VMEM((2, FACE, FACE), BF16),
            field,
            field,
            field,
            pltpu.VMEM((2 * NS, NS), F32),
            pltpu.VMEM((2 * FACE, NS), F32),
            faces,
            faces,
            faces,
            faces,
            pltpu.VMEM((NS, NS), F32),
            pltpu.VMEM((NS, NS), F32),
            pltpu.VMEM((NS, NS), F32),
            pltpu.VMEM((BLOCKS, ROWS, NS), jnp.int32),
            pltpu.VMEM((BLOCKS, ROWS), jnp.int32),
            pltpu.VMEM((FACE, NS), F32),
            pltpu.VMEM((2 * NS, 2 * NS), F32),
            dma((2, 2)),
            dma((2, 2)),
            dma,
            *one_sum,
            *one_sum,
        ],
        compiler_params=pltpu.CompilerParams(
            collective_id=0, has_side_effects=True, vmem_limit_bytes=62 * 1024 * 1024
        ),
    )(*operands)


def body(
    states,
    potential,
    cell_scale,
    stiffness,
    connect,
    face_nodes,
    node_count,
    filter_cut,
    spectrum_top,
):
    return whole(
        lax.axis_size("dom"),
        lax.axis_size("grp"),
        (
            filter_cut,
            spectrum_top,
            node_count,
            states,
            potential.reshape(COUNT // NS, NS),
            cell_scale.reshape(CELLS // NS, NS),
            stiffness,
            connect,
            face_nodes,
        ),
    )


def solution(mesh):
    placed = (
        P(("dom", "grp"), None),
        P(("dom", "grp")),
        P(("dom", "grp")),
        P(),
        P(None, ("dom", "grp")),
        P(None, ("dom", "grp")),
        P(("dom", "grp")),
        P(),
        P(),
    )
    return jax.shard_map(
        body,
        mesh=mesh,
        in_specs=placed,
        out_specs=(P(("dom", "grp"), None), P("grp", None)),
        check_vma=False,
    )
```
